128 devices in a mesh: dom: 16 (over z, x), sub: 8 (over y, core).
Axes of the slice: x: 4, y: 4, z: 4, core: 2. Of those that a mesh axis runs over, the one named last changes fastest.
Arguments:
- tile_blocks: bfloat16 [2048, 18, 192, 192], P(('dom', 'sub')), may hold values from -0.109375 to 0.109375
- neighbours: int32 [2048, 18], P(('dom', 'sub')), may hold values from 0 to 47
- send_groups: int32 [4096], P(('dom', 'sub')), may hold values from 0 to 15
- block_x: float32 [393216, 64], P(('dom', 'sub')), may hold values from -6 to 6
- block_p: float32 [393216, 64], P(('dom', 'sub')), may hold values from -6 to 6
Outputs:
- basis: float32 [393216, 192], P(('dom', 'sub'))
- basis_image: float32 [393216, 192], P(('dom', 'sub'))
- projected: float32 [192, 192], replicated
The draws below stay inside these ranges and needn't reach their ends.
Inputs may be any that keep to these rules, and one draw needn't show every extreme that they name: `neighbours`: each entry indexes the owner's extended group list of 48 entries. `send_groups`: local group indices, 16 for the previous device then 16 for the next, per device.
All inputs are finite; a program needn't handle non-finite values.
Results may differ from the reference program's by a relative error of at most 0.0003.
The reference program's roundings to bfloat16 on the way count: a program that leaves them out, or rounds other values in their place, can miss the bound.
Values may be sent and summed in bfloat16 or wider, within the bound.
No kernel may reach another device: no remote copies, remote signals or barrier semaphores. Data moves between devices by JAX's collectives and lax.ppermute only.
A program may use at most 128 MiB of HBM per device.

```python
import jax
import jax.numpy as jnp
from jax import lax

G_DEV = 16
NB = 18
DOF = 192
BLOCK = 64
BASIS = 192
GROUPS = 2048
ROWS = 393216
SLOTS = 4096
N_DOM = 16
N_SUB = 8


def touch_ends(entries, rng, smallest, high):
    index_at = [jax.random.randint(jax.random.fold_in(rng, axis), (), 0, length) for axis, length in enumerate(entries.shape)]
    longest = entries.shape.index(max(entries.shape))
    beside = index_at[:longest] + [(index_at[longest] + 1) % entries.shape[longest]] + index_at[longest + 1:]
    return entries.at[tuple(index_at)].set(smallest).at[tuple(beside)].set(high)


def levels(stream_key, extent, cuts, low, largest):
    gain, own = 1.0, jax.random.fold_in(stream_key, 6)
    for dim, parts in cuts:
        heights = jnp.exp(jax.random.uniform(jax.random.fold_in(own, dim), (parts,), jnp.float32, low / len(cuts), largest / len(cuts)))
        gain = gain * jnp.repeat(heights, extent[dim] // parts).reshape([-1 if axis == dim else 1 for axis in range(len(extent))])
    return gain


def scatter_about(own_key, extent, deviation, reach, pieces=(), kind=jnp.bfloat16):
    values = jax.random.normal(own_key, extent, jnp.float32) * deviation
    if len(pieces) > 0:
        values = levels(own_key, extent, pieces, -0.22, 0.18) * values
    return jnp.clip(values, min=-reach, max=reach).astype(kind)


def setup_inputs(seed: int = 0) -> dict:
    streams_of = jax.random.split(jax.random.key(seed), 6)
    return {
        "tile_blocks": scatter_about(streams_of[0], (GROUPS, NB, DOF, DOF), (NB * DOF) ** -0.5, 0.109375, ((0, 128),)),
        "neighbours": touch_ends(jax.random.randint(streams_of[1], (GROUPS, NB), 0, 3 * G_DEV), jax.random.fold_in(streams_of[1], 1), 0, (3 * G_DEV) - 1).astype(jnp.int32),
        "send_groups": touch_ends(jax.random.randint(streams_of[2], (SLOTS,), 0, G_DEV), jax.random.fold_in(streams_of[2], 1), 0, G_DEV - 1).astype(jnp.int32),
        "block_x": scatter_about(streams_of[3], (ROWS, BLOCK), 1.0, 6.0, ((0, 128),), jnp.float32),
        "block_p": scatter_about(streams_of[4], (ROWS, BLOCK), 1.0, 6.0, ((0, 128),), jnp.float32),
    }


def apply_operator(tile_blocks, neighbours, send_groups, vectors):
    devices = N_DOM * N_SUB
    columns = vectors.shape[1]
    grouped = vectors.reshape(GROUPS, DOF, columns)
    sends = send_groups.reshape(devices, 2, G_DEV)
    device_ids = jnp.arange(devices, dtype=jnp.int32)
    before_id = jnp.maximum(device_ids - 1, 0)
    after_id = jnp.minimum(device_ids + 1, devices - 1)
    left_ids = ((device_ids - 1)[:, None] * G_DEV + sends[before_id, 1]).astype(jnp.int32)
    own_ids = (device_ids[:, None] * G_DEV + jnp.arange(G_DEV, dtype=jnp.int32)[None, :]).astype(jnp.int32)
    right_ids = ((device_ids + 1)[:, None] * G_DEV + sends[after_id, 0]).astype(jnp.int32)
    extended = jnp.clip(jnp.concatenate([left_ids, own_ids, right_ids], 1), 0, GROUPS - 1)
    left_valid = jnp.broadcast_to((device_ids > 0)[:, None], (devices, G_DEV))
    right_valid = jnp.broadcast_to((device_ids < devices - 1)[:, None], (devices, G_DEV))
    valid = jnp.concatenate([left_valid, jnp.ones((devices, G_DEV), bool), right_valid], 1)
    tiles_dev = tile_blocks.reshape(devices, G_DEV, NB, DOF, DOF)
    links_dev = neighbours.reshape(devices, G_DEV, NB)

    def one_device(index):
        links = links_dev[index]
        source = extended[index][links]
        usable = valid[index][links]
        picked = jnp.where(usable[:, :, None, None], grouped[source], jnp.zeros((), vectors.dtype))
        return jnp.einsum('gkij,gkjc->gic', tiles_dev[index].astype(jnp.float32), picked.astype(jnp.float32))
    result = lax.map(one_device, jnp.arange(devices, dtype=jnp.int32))
    return result.reshape(ROWS, columns)

def reference(tile_blocks, neighbours, send_groups, block_x, block_p):
    highest = lax.Precision.HIGHEST
    x_image = apply_operator(tile_blocks, neighbours, send_groups, block_x.astype(jnp.bfloat16))
    x_gram = jnp.dot(block_x.T, block_x, precision=highest)
    x_cross = jnp.dot(block_x.T, x_image, precision=highest)
    factor = jnp.linalg.cholesky(x_gram)
    quotient = jax.scipy.linalg.cho_solve((factor, True), x_cross)
    residual = x_image - jnp.dot(block_x, quotient, precision=highest)
    stacked = jnp.concatenate([residual, block_p], 1).astype(jnp.bfloat16)
    rp_image = apply_operator(tile_blocks, neighbours, send_groups, stacked)
    search = jnp.concatenate([block_x, residual, block_p], 1)
    search_image = jnp.concatenate([x_image, rp_image], 1)
    total = jnp.float32(ROWS)
    gram = jnp.dot(search.T, search, precision=highest) / total
    lower = jnp.linalg.cholesky(gram)
    inverse = jax.scipy.linalg.solve_triangular(lower, jnp.eye(BASIS, dtype=jnp.float32), lower=True)
    basis = jnp.dot(search, inverse.T, precision=highest)
    basis_image = jnp.dot(search_image, inverse.T, precision=highest)
    projected = jnp.dot(basis.T, basis_image, precision=highest) / total
    return (basis, basis_image, projected)
```

```python
import functools

import jax
import jax.numpy as jnp
from jax import lax
from jax.experimental import pallas as pl
from jax.experimental.pallas import tpu as pltpu
from jax.sharding import PartitionSpec as P

AXES = ("dom", "sub")
HIGHEST = lax.Precision.HIGHEST
MIB = 2**20
NT = (((1,), (1,)), ((), ()))
TN = (((0,), (0,)), ((), ()))
NN = (((1,), (0,)), ((), ()))


def dot32(a, b, dims):
    return lax.dot_general(a, b, dims, precision=HIGHEST, preferred_element_type=jnp.float32)


def split(odd, value, mine, theirs):
    half = value.shape[0] // 2
    mine[...] = jnp.where(odd[:1] > 0, value[half:], value[:half])
    theirs[...] = jnp.where(odd[:1] > 0, value[:half], value[half:])


def join(odd, mine, theirs):
    first = jnp.where(odd[:1] > 0, theirs, mine)
    second = jnp.where(odd[:1] > 0, mine, theirs)
    return jnp.concatenate([first, second], 0)


def all_sum(mine, theirs, sub, dom):
    twin = [(i, i ^ 1) for i in range(sub)]
    mine = mine + lax.ppermute(theirs, "sub", twin)
    for axis, count, flip in (
        ("sub", sub, 2), ("sub", sub, 6), ("dom", dom, 1), ("dom", dom, 3), ("dom", dom, 4), ("dom", dom, 12)
    ):
        mine = mine + lax.ppermute(mine, axis, [(i, i ^ flip) for i in range(count)])
    return mine, lax.ppermute(mine, "sub", twin)


def to_both(block, devices):
    before = lax.ppermute(block, AXES, [(i, i + 1) for i in range(devices - 1)])
    after = lax.ppermute(block, AXES, [(i + 1, i) for i in range(devices - 1)])
    return before, after


def load_kernel(odd, tiles_hbm, x, p, tiles, gram, sems):
    parts = sems.shape[0]
    size = tiles.shape[0] // parts
    copies = [
        pltpu.make_async_copy(tiles_hbm.at[pl.ds(i * size, size)], tiles.at[pl.ds(i * size, size)], sems.at[i])
        for i in range(parts)
    ]
    for copy in copies:
        copy.start()
    both = jnp.concatenate([x[...], p[...]], 0)
    gram[...] = dot32(both, both, NT)
    for copy in copies:
        copy.wait()


def load(odd, tiles, x, p):
    cols = x.shape[0]
    vmem = pl.BlockSpec(memory_space=pltpu.VMEM)
    return pl.pallas_call(
        load_kernel,
        out_shape=(
            pltpu.VMEM(tiles.shape, tiles.dtype),
            jax.ShapeDtypeStruct((2 * cols, 2 * cols), jnp.float32),
        ),
        in_specs=[vmem, pl.BlockSpec(memory_space=pl.ANY), vmem, vmem],
        out_specs=(vmem, vmem),
        scratch_shapes=[pltpu.SemaphoreType.DMA((8,))],
        compiler_params=pltpu.CompilerParams(vmem_limit_bytes=16 * MIB),
        cost_estimate=pl.CostEstimate(flops=200000000, bytes_accessed=30000000, transcendentals=0),
    )(odd, tiles, x, p)


def fill_slabs(slabs, blocks, count, size):
    for place, block in enumerate(blocks):
        for pair in range(count // 2):
            both = block[:, pair * 2 * size : (pair + 1) * 2 * size]
            slabs[place * count + 2 * pair] = both[:, :size]
            slabs[place * count + 2 * pair + 1] = both[:, size:]


def multiply_tiles(nb, table, tiles, slabs, image, count, per):
    size = tiles.shape[2]

    def step(pair, carry):
        wide = []
        for half in range(per):
            group = pair * per + half
            total = None
            for k in range(tiles.shape[1]):
                slab = slabs[table[nb[group, k]]]
                part = lax.dot_general(tiles[group, k], slab, NT, preferred_element_type=jnp.float32)
                total = part if total is None else total + part
            wide.append(total.T)
        width = per * size
        image[:, pl.ds(pl.multiple_of(pair * width, width), width)] = jnp.concatenate(wide, 1)
        return carry

    lax.fori_loop(0, count // per, step, 0)


def first_kernel(
    per, nb, table, odd, tiles, own, before, after, x, p, gram, x_image, p_image, mine, theirs, slabs, images
):
    count, size, cols = tiles.shape[0], tiles.shape[2], x.shape[0]
    fill_slabs(slabs, (before, own, after), count, size)
    multiply_tiles(nb, table, tiles, slabs, images, count, per)
    image = images[:cols]
    x_image[...] = image
    p_image[...] = images[cols:]
    cross = dot32(jnp.concatenate([x[...], image, p[...]], 0), image, NT)
    g = gram[...]
    left = jnp.concatenate([g[:cols, :cols], g[cols:, :cols], g[cols:, cols:]], 0)
    split(odd, jnp.concatenate([left, cross], 1), mine, theirs)


def half_of(cols):
    return jax.ShapeDtypeStruct((3 * cols // 2, 2 * cols), jnp.float32)


def first_images(nb, table, odd, tiles, own, before, after, x, p, gram):
    count, size, cols = tiles.shape[0], tiles.shape[2], x.shape[0]
    vmem = pl.BlockSpec(memory_space=pltpu.VMEM)
    smem = pl.BlockSpec(memory_space=pltpu.SMEM)
    return pl.pallas_call(
        functools.partial(first_kernel, 4),
        out_shape=(
            jax.ShapeDtypeStruct(x.shape, jnp.float32),
            jax.ShapeDtypeStruct(x.shape, jnp.float32),
            half_of(cols),
            half_of(cols),
        ),
        in_specs=[smem, smem] + [vmem] * 8,
        out_specs=(vmem,) * 4,
        scratch_shapes=[
            pltpu.VMEM((3 * count, 2 * cols, size), jnp.bfloat16),
            pltpu.VMEM((2 * cols, x.shape[1]), jnp.float32),
        ],
        compiler_params=pltpu.CompilerParams(vmem_limit_bytes=16 * MIB),
        cost_estimate=pl.CostEstimate(flops=10000000000, bytes_accessed=4000000, transcendentals=0),
    )(nb, table, odd, pltpu.with_memory_space_constraint(tiles, pltpu.VMEM), own, before, after, x, p, gram)


def middle_kernel(x, r, p, p_image, packed):
    packed[...] = dot32(jnp.concatenate([x[...], r[...], p[...]], 0), p_image[...], NT)


def middle_products(x, r, p, p_image):
    vmem = pl.BlockSpec(memory_space=pltpu.VMEM)
    return pl.pallas_call(
        middle_kernel,
        out_shape=jax.ShapeDtypeStruct((3 * x.shape[0], x.shape[0]), jnp.float32),
        in_specs=[vmem] * 4,
        out_specs=vmem,
        compiler_params=pltpu.CompilerParams(vmem_limit_bytes=4 * MIB),
        cost_estimate=pl.CostEstimate(flops=1500000000, bytes_accessed=3000000, transcendentals=0),
    )(x, r, p, p_image)


def second_kernel(
    per, nb, table, odd, tiles, own, before, after, x, r, p, middle, r_image, mine, theirs, slabs
):
    count, size = tiles.shape[0], tiles.shape[2]
    fill_slabs(slabs, (before, own, after), count, size)
    multiply_tiles(nb, table, tiles, slabs, r_image, count, per)
    cross = dot32(jnp.concatenate([x[...], r[...], p[...]], 0), r_image[...], NT)
    split(odd, jnp.concatenate([cross, middle[...]], 1), mine, theirs)


def second_images(nb, table, odd, tiles, own, before, after, x, r, p, middle):
    count, size, cols = tiles.shape[0], tiles.shape[2], x.shape[0]
    vmem = pl.BlockSpec(memory_space=pltpu.VMEM)
    smem = pl.BlockSpec(memory_space=pltpu.SMEM)
    return pl.pallas_call(
        functools.partial(second_kernel, 4),
        out_shape=(
            jax.ShapeDtypeStruct(x.shape, jnp.float32),
            half_of(cols),
            half_of(cols),
        ),
        in_specs=[smem, smem] + [vmem] * 9,
        out_specs=(vmem,) * 3,
        scratch_shapes=[pltpu.VMEM((3 * count, cols, size), jnp.bfloat16)],
        compiler_params=pltpu.CompilerParams(vmem_limit_bytes=16 * MIB),
        cost_estimate=pl.CostEstimate(flops=10000000000, bytes_accessed=4000000, transcendentals=0),
    )(nb, table, odd, pltpu.with_memory_space_constraint(tiles, pltpu.VMEM), own, before, after, x, r, p, middle)


def cholesky_inverse(a):
    n, step = a.shape[0], 8
    rows = lax.broadcasted_iota(jnp.int32, (step, 2 * n), 0)
    lanes = lax.broadcasted_iota(jnp.int32, (n, n), 1)
    unit = (lanes == lax.broadcasted_iota(jnp.int32, (n, n), 0)).astype(jnp.float32)
    m = jnp.concatenate([a, unit], 1)
    bands = [m[i : i + step] for i in range(0, n, step)]
    pivots = []
    for at in range(n // step):
        live = range(at, n // step)
        columns = [
            {t: jnp.broadcast_to(bands[t][:, at * step + i : at * step + i + 1], (step, 2 * n)) for t in live}
            for i in range(step)
        ]
        for i in range(step):
            pivot = columns[i][at][i : i + 1]
            pivots.append(pivot)
            over = 1.0 / pivot
            row = bands[at][i : i + 1]
            factor = {t: columns[i][t] * over for t in live}
            factor[at] = jnp.where(rows > i, factor[at], 0.0)
            for later in range(i + 1, step):
                entry = columns[later][at][i : i + 1]
                for t in live:
                    columns[later][t] = columns[later][t] - factor[t] * entry
            for t in live:
                bands[t] = bands[t] - factor[t] * row
    scale = jnp.concatenate(pivots, 0)
    return (jnp.concatenate(bands, 0) * (1.0 / jnp.sqrt(scale)))[:, n:]


def residual_kernel(odd, mine, theirs, x, x_image, packed, quotient, inverse, residual, rounded):
    cols = x.shape[0]
    packed[...] = join(odd, mine[...], theirs[...])
    gram, cross = packed[:cols, :cols], packed[:cols, cols:]
    w = cholesky_inverse(gram)
    inverse[...] = w
    q = dot32(w, dot32(w, cross, NN), TN)
    quotient[...] = q
    r = x_image[...] - dot32(q, x[...], TN)
    residual[...] = r
    rounded[...] = r.astype(jnp.bfloat16)


def residual_of(odd, mine, theirs, x, x_image):
    cols = x.shape[0]
    vmem = pl.BlockSpec(memory_space=pltpu.VMEM)
    square = jax.ShapeDtypeStruct((cols, cols), jnp.float32)
    return pl.pallas_call(
        residual_kernel,
        out_shape=(
            jax.ShapeDtypeStruct((3 * cols, 2 * cols), jnp.float32),
            square,
            square,
            jax.ShapeDtypeStruct(x.shape, jnp.float32),
            jax.ShapeDtypeStruct(x.shape, jnp.bfloat16),
        ),
        in_specs=[vmem] * 5,
        out_specs=(vmem,) * 5,
        compiler_params=pltpu.CompilerParams(vmem_limit_bytes=4 * MIB),
        cost_estimate=pl.CostEstimate(flops=3000000000, bytes_accessed=3000000, transcendentals=0),
    )(odd, mine, theirs, x, x_image)


def factor_kernel(total, packed, quotient, x_inverse, inverse, r_cross):
    c = quotient.shape[0]
    q = quotient[...]
    xx, px, pp = packed[:c, :c], packed[c : 2 * c, :c], packed[2 * c :, :c]
    xi, ii, pi = packed[:c, c:], packed[c : 2 * c, c:], packed[2 * c :, c:]
    rx = xi.T - dot32(q, xx, TN)
    ri = ii - dot32(q, xi, TN)
    rr = ri - dot32(rx, q, NN)
    pr = pi - dot32(px, q, NN)
    r_cross[...] = ri
    scale = 1.0 / total
    w1 = x_inverse[...] * (total**0.5)
    l21, l31 = dot32(rx * scale, w1, NT), dot32(px * scale, w1, NT)
    w2 = cholesky_inverse(rr * scale - dot32(l21, l21, NT))
    l32 = dot32(pr * scale - dot32(l31, l21, NT), w2, NT)
    w3 = cholesky_inverse(pp * scale - dot32(l31, l31, NT) - dot32(l32, l32, NT))
    w21 = -dot32(w2, dot32(l21, w1, NN), NN)
    w32 = -dot32(w3, dot32(l32, w2, NN), NN)
    w31 = -dot32(w3, dot32(l31, w1, NN) + dot32(l32, w21, NN), NN)
    zero = jnp.zeros_like(w1)
    inverse[...] = jnp.concatenate(
        [
            jnp.concatenate([w1, zero, zero], 1),
            jnp.concatenate([w21, w2, zero], 1),
            jnp.concatenate([w31, w32, w3], 1),
        ],
        0,
    )


def factor(total, packed, quotient, x_inverse):
    c = quotient.shape[0]
    vmem = pl.BlockSpec(memory_space=pltpu.VMEM)
    return pl.pallas_call(
        functools.partial(factor_kernel, total),
        out_shape=(
            jax.ShapeDtypeStruct((3 * c, 3 * c), jnp.float32),
            jax.ShapeDtypeStruct((c, c), jnp.float32),
        ),
        in_specs=[vmem] * 3,
        out_specs=(vmem,) * 2,
        compiler_params=pltpu.CompilerParams(vmem_limit_bytes=16 * MIB),
        cost_estimate=pl.CostEstimate(flops=3000000000, bytes_accessed=3000000, transcendentals=0),
    )(packed, quotient, x_inverse)


def basis_kernel(inverse, x, r, p, x_image, r_image, p_image, basis, basis_image):
    w = inverse[...]
    basis[...] = dot32(w, jnp.concatenate([x[...], r[...], p[...]], 0), NN)
    basis_image[...] = dot32(w, jnp.concatenate([x_image[...], r_image[...], p_image[...]], 0), NN)


def bases(inverse, *blocks):
    width, rows = inverse.shape[0], blocks[0].shape[1]
    cols = blocks[0].shape[0]
    tile = 512
    block = pl.BlockSpec((cols, tile), lambda i: (0, i))
    out = pl.BlockSpec((width, tile), lambda i: (0, i))
    return pl.pallas_call(
        basis_kernel,
        grid=(rows // tile,),
        out_shape=(jax.ShapeDtypeStruct((width, rows), jnp.float32),) * 2,
        in_specs=[pl.BlockSpec((width, width), lambda i: (0, 0))] + [block] * 6,
        out_specs=(out, out),
        compiler_params=pltpu.CompilerParams(vmem_limit_bytes=16 * MIB),
        cost_estimate=pl.CostEstimate(flops=2700000000, bytes_accessed=10000000, transcendentals=0),
    )(inverse, *blocks)


def project_kernel(total, odd, inverse, packed, r_cross, mine, theirs, projected):
    c = r_cross.shape[0]
    left = jnp.concatenate([packed[:c, c:], r_cross[...], packed[2 * c :, c:]], 0)
    w = inverse[...]
    cross = jnp.concatenate([left, join(odd, mine[...], theirs[...])], 1)
    projected[...] = dot32(dot32(w, cross, NN), w, NT) * (1.0 / total)


def project(total, odd, inverse, packed, r_cross, mine, theirs):
    vmem = pl.BlockSpec(memory_space=pltpu.VMEM)
    return pl.pallas_call(
        functools.partial(project_kernel, total),
        out_shape=jax.ShapeDtypeStruct(inverse.shape, jnp.float32),
        in_specs=[vmem] * 6,
        out_specs=vmem,
        compiler_params=pltpu.CompilerParams(vmem_limit_bytes=16 * MIB),
    )(odd, inverse, packed, r_cross, mine, theirs)


def shards(sub, dom, tile_blocks, neighbours, send_groups, block_x, block_p):
    devices = sub * dom
    count, rows, cols = tile_blocks.shape[0], block_x.shape[0], block_x.shape[1]
    total = float(rows * devices)
    x, p = block_x.T, block_p.T
    lists = jnp.pad(send_groups.astype(jnp.bfloat16)[None], ((0, 2 * cols - 1), (0, 128 - 2 * count)))
    both = jnp.concatenate([jnp.concatenate([x, p], 0).astype(jnp.bfloat16), lists], 1)
    before, after = to_both(both, devices)
    table = jnp.concatenate(
        [
            before[0, rows + count : rows + 2 * count].astype(jnp.int32),
            jnp.arange(count, 2 * count, dtype=jnp.int32),
            after[0, rows : rows + count].astype(jnp.int32) + 2 * count,
        ]
    )
    odd = jnp.broadcast_to(lax.axis_index("sub") % 2, (8, 2 * cols)).astype(jnp.float32)
    tiles, gram = load(odd, tile_blocks, x, p)
    x_image, p_image, *halves = first_images(neighbours, table, odd, tiles, both, before, after, x, p, gram)
    halves = all_sum(*halves, sub, dom)
    packed, quotient, x_inverse, residual, r_round = residual_of(odd, *halves, x, x_image)
    r_before, r_after = to_both(r_round, devices)
    middle = middle_products(x, residual, p, p_image)
    r_image, *halves = second_images(
        neighbours, table, odd, tiles, r_round, r_before, r_after, x, residual, p, middle
    )
    halves = all_sum(*halves, sub, dom)
    inverse, r_cross = factor(total, packed, quotient, x_inverse)
    basis, basis_image = bases(inverse, x, residual, p, x_image, r_image, p_image)
    projected = project(total, odd, inverse, packed, r_cross, *halves)
    return basis.T, basis_image.T, projected


def solution(mesh):
    placed = (
        P(AXES, None, None, None),
        P(AXES, None),
        P(AXES),
        P(AXES, None),
        P(AXES, None),
    )
    return jax.shard_map(
        functools.partial(shards, mesh.shape["sub"], mesh.shape["dom"]),
        mesh=mesh,
        in_specs=placed,
        out_specs=(P(AXES, None), P(AXES, None), P()),
        check_vma=False,
    )
```

```python
import functools

import jax
import jax.numpy as jnp
from jax import lax
from jax.experimental import pallas as pl
from jax.experimental.pallas import tpu as pltpu
from jax.sharding import PartitionSpec as P

AXES = ("dom", "sub")
HIGHEST = lax.Precision.HIGHEST
MIB = 2**20
NT = (((1,), (1,)), ((), ()))
TN = (((0,), (0,)), ((), ()))
NN = (((1,), (0,)), ((), ()))
ZEROS = jax.ShapeDtypeStruct((8, 128), jnp.float32)


def dot32(a, b, dims):
    return lax.dot_general(a, b, dims, precision=HIGHEST, preferred_element_type=jnp.float32)


def split(odd, value, mine, theirs):
    half = value.shape[0] // 2
    mine[...] = jnp.where(odd[:1] > 0, value[half:], value[:half])
    theirs[...] = jnp.where(odd[:1] > 0, value[:half], value[half:])


def join(odd, mine, theirs):
    first = jnp.where(odd[:1] > 0, theirs, mine)
    second = jnp.where(odd[:1] > 0, mine, theirs)
    return jnp.concatenate([first, second], 0)


def all_sum(mine, theirs, sub, dom, work=()):
    twin = [(i, i ^ 1) for i in range(sub)]
    mine = mine + lax.ppermute(theirs, "sub", twin)
    steps = [
        ("dom", dom, 4), ("dom", dom, 12), ("dom", dom, 1), ("dom", dom, 3), ("sub", sub, 2), ("sub", sub, 6)
    ]
    for at, (axis, count, flip) in enumerate(steps):
        got = lax.ppermute(mine, axis, [(i, i ^ flip) for i in range(count)])
        if at < len(work) and work[at] is not None:
            zeros = work[at](mine)
            mine = (mine + got) + zeros[:1]
        else:
            mine = mine + got
    return mine, lax.ppermute(mine, "sub", twin)


def neighbour_blocks(block, sub, devices):
    pairs = [(i, i + 1) for i in range(1, devices - 1, 2)]
    other = lax.ppermute(block, AXES, pairs + [(j, i) for i, j in pairs])
    twin = lax.ppermute(block, "sub", [(i, i ^ 1) for i in range(sub)])
    return twin, other


def load_kernel(odd, tiles_hbm, x, p, tiles, gram, sems):
    parts = sems.shape[0]
    size = tiles.shape[0] // parts
    copies = [
        pltpu.make_async_copy(tiles_hbm.at[pl.ds(i * size, size)], tiles.at[pl.ds(i * size, size)], sems.at[i])
        for i in range(parts)
    ]
    for copy in copies:
        copy.start()
    both = jnp.concatenate([x[...], p[...]], 0)
    gram[...] = dot32(both, both, NT)
    for copy in copies:
        copy.wait()


def load(odd, tiles, x, p):
    cols = x.shape[0]
    vmem = pl.BlockSpec(memory_space=pltpu.VMEM)
    return pl.pallas_call(
        load_kernel,
        out_shape=(
            pltpu.VMEM(tiles.shape, tiles.dtype),
            jax.ShapeDtypeStruct((2 * cols, 2 * cols), jnp.float32),
        ),
        in_specs=[vmem, pl.BlockSpec(memory_space=pl.ANY), vmem, vmem],
        out_specs=(vmem, vmem),
        scratch_shapes=[pltpu.SemaphoreType.DMA((8,))],
        compiler_params=pltpu.CompilerParams(vmem_limit_bytes=16 * MIB),
        cost_estimate=pl.CostEstimate(flops=200000000, bytes_accessed=30000000, transcendentals=0),
    )(odd, tiles, x, p)


def fill_slabs(slabs, blocks, count, size):
    for place, block in enumerate(blocks):
        for pair in range(count // 2):
            both = block[:, pair * 2 * size : (pair + 1) * 2 * size]
            slabs[place * count + 2 * pair] = both[:, :size]
            slabs[place * count + 2 * pair + 1] = both[:, size:]


def multiply_tiles(nb, table, tiles, slabs, image, count, per):
    size = tiles.shape[2]

    def step(pair, carry):
        wide = []
        for half in range(per):
            group = pair * per + half
            total = None
            for k in range(tiles.shape[1]):
                slab = slabs[table[nb[group, k]]]
                part = lax.dot_general(tiles[group, k], slab, NT, preferred_element_type=jnp.float32)
                total = part if total is None else total + part
            wide.append(total.T)
        width = per * size
        image[:, pl.ds(pl.multiple_of(pair * width, width), width)] = jnp.concatenate(wide, 1)
        return carry

    lax.fori_loop(0, count // per, step, 0)


def first_kernel(
    per, nb, table, odd, tiles, own, twin, other, x, p, gram, x_image, p_image, mine, theirs, slabs, images
):
    count, size, cols = tiles.shape[0], tiles.shape[2], x.shape[0]
    fill_slabs(slabs, (own, twin, other), count, size)
    multiply_tiles(nb, table, tiles, slabs, images, count, per)
    image = images[:cols]
    x_image[...] = image
    p_image[...] = images[cols:]
    cross = dot32(jnp.concatenate([x[...], image, p[...]], 0), image, NT)
    g = gram[...]
    left = jnp.concatenate([g[:cols, :cols], g[cols:, :cols], g[cols:, cols:]], 0)
    split(odd, jnp.concatenate([left, cross], 1), mine, theirs)


def half_of(cols):
    return jax.ShapeDtypeStruct((3 * cols // 2, 2 * cols), jnp.float32)


def first_images(nb, table, odd, tiles, own, twin, other, x, p, gram):
    count, size, cols = tiles.shape[0], tiles.shape[2], x.shape[0]
    vmem = pl.BlockSpec(memory_space=pltpu.VMEM)
    smem = pl.BlockSpec(memory_space=pltpu.SMEM)
    return pl.pallas_call(
        functools.partial(first_kernel, 4),
        out_shape=(
            jax.ShapeDtypeStruct(x.shape, jnp.float32),
            jax.ShapeDtypeStruct(x.shape, jnp.float32),
            half_of(cols),
            half_of(cols),
        ),
        in_specs=[smem, smem] + [vmem] * 8,
        out_specs=(vmem,) * 4,
        scratch_shapes=[
            pltpu.VMEM((3 * count, 2 * cols, size), jnp.bfloat16),
            pltpu.VMEM((2 * cols, x.shape[1]), jnp.float32),
        ],
        compiler_params=pltpu.CompilerParams(vmem_limit_bytes=16 * MIB),
        cost_estimate=pl.CostEstimate(flops=10000000000, bytes_accessed=4000000, transcendentals=0),
    )(nb, table, odd, pltpu.with_memory_space_constraint(tiles, pltpu.VMEM), own, twin, other, x, p, gram)


def middle_kernel(sent, x, x_image, p, p_image, packed, zeros):
    zeros[...] = jnp.zeros_like(zeros)
    packed[...] = dot32(jnp.concatenate([x[...], x_image[...], p[...]], 0), p_image[...], NT)


def middle_products(sent, x, x_image, p, p_image):
    vmem = pl.BlockSpec(memory_space=pltpu.VMEM)
    return pl.pallas_call(
        middle_kernel,
        out_shape=(jax.ShapeDtypeStruct((3 * x.shape[0], x.shape[0]), jnp.float32), ZEROS),
        in_specs=[pl.BlockSpec(memory_space=pl.ANY)] + [vmem] * 4,
        out_specs=(vmem, vmem),
        compiler_params=pltpu.CompilerParams(vmem_limit_bytes=4 * MIB),
        cost_estimate=pl.CostEstimate(flops=1500000000, bytes_accessed=3000000, transcendentals=0),
    )(sent, x, x_image, p, p_image)


def second_kernel(
    per, nb, table, odd, tiles, own, twin, other, x, r, p, middle, quotient, parts, r_image, mine, theirs, slabs
):
    count, size = tiles.shape[0], tiles.shape[2]
    fill_slabs(slabs, (own, twin, other), count, size)
    multiply_tiles(nb, table, tiles, slabs, r_image, count, per)
    cross = dot32(jnp.concatenate([x[...], r[...], p[...]], 0), r_image[...], NT)
    c = x.shape[0]
    xp, ip, pp = middle[:c], middle[c : 2 * c], middle[2 * c :]
    rp = ip - dot32(quotient[...], xp, TN)
    split(odd, jnp.concatenate([cross, jnp.concatenate([xp, rp, pp], 0)], 1), mine, theirs)


def second_images(nb, table, odd, tiles, own, twin, other, x, r, p, middle, quotient, parts):
    count, size, cols = tiles.shape[0], tiles.shape[2], x.shape[0]
    vmem = pl.BlockSpec(memory_space=pltpu.VMEM)
    smem = pl.BlockSpec(memory_space=pltpu.SMEM)
    return pl.pallas_call(
        functools.partial(second_kernel, 4),
        out_shape=(
            jax.ShapeDtypeStruct(x.shape, jnp.float32),
            half_of(cols),
            half_of(cols),
        ),
        in_specs=[smem, smem] + [vmem] * 10 + [pl.BlockSpec(memory_space=pl.ANY)],
        out_specs=(vmem,) * 3,
        scratch_shapes=[pltpu.VMEM((3 * count, cols, size), jnp.bfloat16)],
        compiler_params=pltpu.CompilerParams(vmem_limit_bytes=16 * MIB),
        cost_estimate=pl.CostEstimate(flops=10000000000, bytes_accessed=4000000, transcendentals=0),
    )(nb, table, odd, pltpu.with_memory_space_constraint(tiles, pltpu.VMEM), own, twin, other, x, r, p, middle, quotient, parts)


def cholesky_inverse(a):
    n, step = a.shape[0], 8
    rows = lax.broadcasted_iota(jnp.int32, (step, 2 * n), 0)
    lanes = lax.broadcasted_iota(jnp.int32, (n, n), 1)
    unit = (lanes == lax.broadcasted_iota(jnp.int32, (n, n), 0)).astype(jnp.float32)
    m = jnp.concatenate([a, unit], 1)
    bands = [m[i : i + step] for i in range(0, n, step)]
    pivots = []
    for at in range(n // step):
        live = range(at, n // step)
        columns = [
            {t: jnp.broadcast_to(bands[t][:, at * step + i : at * step + i + 1], (step, 2 * n)) for t in live}
            for i in range(step)
        ]
        for i in range(step):
            pivot = columns[i][at][i : i + 1]
            pivots.append(pivot)
            over = 1.0 / pivot
            row = bands[at][i : i + 1]
            factor = {t: columns[i][t] * over for t in live}
            factor[at] = jnp.where(rows > i, factor[at], 0.0)
            for later in range(i + 1, step):
                entry = columns[later][at][i : i + 1]
                for t in live:
                    columns[later][t] = columns[later][t] - factor[t] * entry
            for t in live:
                bands[t] = bands[t] - factor[t] * row
    scale = jnp.concatenate(pivots, 0)
    return (jnp.concatenate(bands, 0) * (1.0 / jnp.sqrt(scale)))[:, n:]


def residual_kernel(odd, mine, theirs, x, x_image, packed, quotient, inverse, residual, rounded):
    cols = x.shape[0]
    packed[...] = join(odd, mine[...], theirs[...])
    gram, cross = packed[:cols, :cols], packed[:cols, cols:]
    w = cholesky_inverse(gram)
    inverse[...] = w
    q = dot32(w, dot32(w, cross, NN), TN)
    quotient[...] = q
    r = x_image[...] - dot32(q, x[...], TN)
    residual[...] = r
    rounded[...] = r.astype(jnp.bfloat16)


def residual_of(odd, mine, theirs, x, x_image):
    cols = x.shape[0]
    vmem = pl.BlockSpec(memory_space=pltpu.VMEM)
    square = jax.ShapeDtypeStruct((cols, cols), jnp.float32)
    return pl.pallas_call(
        residual_kernel,
        out_shape=(
            jax.ShapeDtypeStruct((3 * cols, 2 * cols), jnp.float32),
            square,
            square,
            jax.ShapeDtypeStruct(x.shape, jnp.float32),
            jax.ShapeDtypeStruct(x.shape, jnp.bfloat16),
        ),
        in_specs=[vmem] * 5,
        out_specs=(vmem,) * 5,
        compiler_params=pltpu.CompilerParams(vmem_limit_bytes=4 * MIB),
        cost_estimate=pl.CostEstimate(flops=3000000000, bytes_accessed=3000000, transcendentals=0),
    )(odd, mine, theirs, x, x_image)


def factor_kernel(total, packed, quotient, x_inverse, parts):
    c = quotient.shape[0]
    q = quotient[...]
    xx, px, pp = packed[:c, :c], packed[c : 2 * c, :c], packed[2 * c :, :c]
    xi, ii, pi = packed[:c, c:], packed[c : 2 * c, c:], packed[2 * c :, c:]
    rx = xi.T - dot32(q, xx, TN)
    ri = ii - dot32(q, xi, TN)
    rr = ri - dot32(rx, q, NN)
    pr = pi - dot32(px, q, NN)
    scale = 1.0 / total
    w1 = x_inverse[...] * (total**0.5)
    l21, l31 = dot32(rx * scale, w1, NT), dot32(px * scale, w1, NT)
    w2 = cholesky_inverse(rr * scale - dot32(l21, l21, NT))
    l32 = dot32(pr * scale - dot32(l31, l21, NT), w2, NT)
    last = pp * scale - dot32(l31, l31, NT) - dot32(l32, l32, NT)
    for at, part in enumerate((w1, w2, l21, l31, l32, last, ri)):
        parts[at] = part


def factor(total, packed, quotient, x_inverse):
    c = quotient.shape[0]
    vmem = pl.BlockSpec(memory_space=pltpu.VMEM)
    return pl.pallas_call(
        functools.partial(factor_kernel, total),
        out_shape=jax.ShapeDtypeStruct((7, c, c), jnp.float32),
        in_specs=[vmem] * 3,
        out_specs=vmem,
        compiler_params=pltpu.CompilerParams(vmem_limit_bytes=4 * MIB),
        cost_estimate=pl.CostEstimate(flops=2000000000, bytes_accessed=3000000, transcendentals=0),
    )(packed, quotient, x_inverse)


def inverse_kernel(sent, parts, inverse, zeros):
    zeros[...] = jnp.zeros_like(zeros)
    w1, w2, l21, l31, l32 = parts[0], parts[1], parts[2], parts[3], parts[4]
    w21 = -dot32(w2, dot32(l21, w1, NN), NN)
    below = dot32(l31, w1, NN) + dot32(l32, w21, NN)
    beside = dot32(l32, w2, NN)
    w3 = cholesky_inverse(parts[5])
    w3_below = -dot32(w3, jnp.concatenate([below, beside], 1), NN)
    zero = jnp.zeros_like(w1)
    inverse[...] = jnp.concatenate(
        [
            jnp.concatenate([w1, zero, zero], 1),
            jnp.concatenate([w21, w2, zero], 1),
            jnp.concatenate([w3_below, w3], 1),
        ],
        0,
    )


def inverse_of(sent, parts):
    width = 3 * parts.shape[1]
    vmem = pl.BlockSpec(memory_space=pltpu.VMEM)
    return pl.pallas_call(
        inverse_kernel,
        out_shape=(jax.ShapeDtypeStruct((width, width), jnp.float32), ZEROS),
        in_specs=[pl.BlockSpec(memory_space=pl.ANY), vmem],
        out_specs=(vmem, vmem),
        compiler_params=pltpu.CompilerParams(vmem_limit_bytes=4 * MIB),
        cost_estimate=pl.CostEstimate(flops=2000000000, bytes_accessed=3000000, transcendentals=0),
    )(sent, parts)


def basis_kernel(extra, sent, inverse, x, r, p, x_image, r_image, p_image, *rest):
    basis, basis_image, zeros = rest[extra:]
    zeros[...] = jnp.zeros_like(zeros)
    w = inverse[...]
    basis[...] = dot32(w, jnp.concatenate([x[...], r[...], p[...]], 0), NN)
    basis_image[...] = dot32(w, jnp.concatenate([x_image[...], r_image[...], p_image[...]], 0), NN)


def bases(part, parts, sent, inverse, blocks, done):
    width, rows = inverse.shape[0], blocks[0].shape[1]
    cols = blocks[0].shape[0]
    tile = 384
    steps = rows // tile // parts
    first = part * steps
    whole = pl.BlockSpec(memory_space=pl.ANY)
    block = pl.BlockSpec((cols, tile), lambda i: (0, first + i))
    out = pl.BlockSpec((width, tile), lambda i: (0, first + i))
    return pl.pallas_call(
        functools.partial(basis_kernel, len(done)),
        grid=(steps,),
        out_shape=(jax.ShapeDtypeStruct((width, rows), jnp.float32),) * 2 + (ZEROS,),
        in_specs=[whole, pl.BlockSpec((width, width), lambda i: (0, 0))] + [block] * 6 + [whole] * len(done),
        out_specs=(out, out, pl.BlockSpec((8, 128), lambda i: (0, 0))),
        input_output_aliases={8 + i: i for i in range(len(done))},
        compiler_params=pltpu.CompilerParams(vmem_limit_bytes=12 * MIB),
        cost_estimate=pl.CostEstimate(flops=2000000000, bytes_accessed=3000000, transcendentals=0),
    )(sent, inverse, *blocks, *done)


def project_kernel(total, odd, inverse, packed, parts, mine, theirs, projected):
    c = parts.shape[1]
    left = jnp.concatenate([packed[:c, c:], parts[6], packed[2 * c :, c:]], 0)
    w = inverse[...]
    cross = jnp.concatenate([left, join(odd, mine[...], theirs[...])], 1)
    projected[...] = dot32(dot32(w, cross, NN), w, NT) * (1.0 / total)


def project(total, odd, inverse, packed, parts, mine, theirs):
    vmem = pl.BlockSpec(memory_space=pltpu.VMEM)
    return pl.pallas_call(
        functools.partial(project_kernel, total),
        out_shape=jax.ShapeDtypeStruct(inverse.shape, jnp.float32),
        in_specs=[vmem] * 6,
        out_specs=vmem,
        compiler_params=pltpu.CompilerParams(vmem_limit_bytes=16 * MIB),
    )(odd, inverse, packed, parts, mine, theirs)


def shards(sub, dom, tile_blocks, neighbours, send_groups, block_x, block_p):
    devices = sub * dom
    count, rows, cols = tile_blocks.shape[0], block_x.shape[0], block_x.shape[1]
    total = float(rows * devices)
    x, p = block_x.T, block_p.T
    lists = jnp.pad(send_groups.astype(jnp.bfloat16)[None], ((0, 2 * cols - 1), (0, 128 - 2 * count)))
    both = jnp.concatenate([jnp.concatenate([x, p], 0).astype(jnp.bfloat16), lists], 1)
    odd = jnp.broadcast_to(lax.axis_index("sub") % 2, (8, 2 * cols)).astype(jnp.float32)
    twin, other = neighbour_blocks(both, sub, devices)
    twin_list = twin[0, rows : rows + 2 * count].astype(jnp.int32) + count
    other_list = other[0, rows : rows + 2 * count].astype(jnp.int32) + 2 * count
    first_half = odd[0, :count] > 0
    table = jnp.concatenate(
        [
            jnp.where(first_half, twin_list[count:], other_list[count:]),
            jnp.arange(count, dtype=jnp.int32),
            jnp.where(first_half, other_list[:count], twin_list[:count]),
        ]
    )
    tiles, gram = load(odd, tile_blocks, x, p)
    x_image, p_image, *halves = first_images(neighbours, table, odd, tiles, both, twin, other, x, p, gram)
    made = {}

    def step(name, make):
        def run(sent):
            *values, zeros = make(sent)
            made[name] = values
            return zeros

        return run

    halves = all_sum(
        *halves, sub, dom, [step("middle", lambda sent: middle_products(sent, x, x_image, p, p_image))]
    )
    packed, quotient, x_inverse, residual, r_round = residual_of(odd, *halves, x, x_image)
    r_twin, r_other = neighbour_blocks(r_round, sub, devices)
    parts = factor(total, packed, quotient, x_inverse)
    r_image, *halves = second_images(
        neighbours, table, odd, tiles, r_round, r_twin, r_other, x, residual, p, made["middle"][0], quotient, parts
    )
    blocks = (x, residual, p, x_image, r_image, p_image)
    made["bases"] = []
    pieces = 4
    work = [
        step("inverse", lambda sent: inverse_of(sent, parts)),
    ]
    for piece in range(pieces):
        work.append(
            step(
                "bases",
                lambda sent, piece=piece: bases(piece, pieces, sent, made["inverse"][0], blocks, made["bases"]),
            )
        )
    halves = all_sum(*halves, sub, dom, work)
    basis, basis_image = made["bases"]
    projected = project(total, odd, made["inverse"][0], packed, parts, *halves)
    return basis.T, basis_image.T, projected


def solution(mesh):
    placed = (
        P(AXES, None, None, None),
        P(AXES, None),
        P(AXES),
        P(AXES, None),
        P(AXES, None),
    )
    return jax.shard_map(
        functools.partial(shards, mesh.shape["sub"], mesh.shape["dom"]),
        mesh=mesh,
        in_specs=placed,
        out_specs=(P(AXES, None), P(AXES, None), P()),
        check_vma=False,
    )
```

```python
import functools

import jax
import jax.numpy as jnp
from jax import lax
from jax.experimental import pallas as pl
from jax.experimental.pallas import tpu as pltpu
from jax.sharding import PartitionSpec as P

AXES = ("dom", "sub")
HIGHEST = lax.Precision.HIGHEST
MIB = 2**20
NT = (((1,), (1,)), ((), ()))
TN = (((0,), (0,)), ((), ()))
NN = (((1,), (0,)), ((), ()))
ZEROS = jax.ShapeDtypeStruct((8, 128), jnp.float32)


def dot32(a, b, dims):
    return lax.dot_general(a, b, dims, precision=HIGHEST, preferred_element_type=jnp.float32)


def halves_of(a):
    high = a.astype(jnp.bfloat16)
    return high, (a - high.astype(jnp.float32)).astype(jnp.bfloat16)


def dot16(a, b, dims):
    (a_high, a_low), (b_high, b_low) = halves_of(a), halves_of(b)
    dot = functools.partial(lax.dot_general, dimension_numbers=dims, preferred_element_type=jnp.float32)
    return dot(a_high, b_high) + (dot(a_high, b_low) + dot(a_low, b_high))


def split(odd, value, mine, theirs):
    half = value.shape[0] // 2
    mine[...] = jnp.where(odd[:1] > 0, value[half:], value[:half])
    theirs[...] = jnp.where(odd[:1] > 0, value[:half], value[half:])


def join(odd, mine, theirs):
    first = jnp.where(odd[:1] > 0, theirs, mine)
    second = jnp.where(odd[:1] > 0, mine, theirs)
    return jnp.concatenate([first, second], 0)


def all_sum(mine, theirs, sub, dom, work=()):
    twin = [(i, i ^ 1) for i in range(sub)]
    mine = mine + lax.ppermute(theirs, "sub", twin)
    y, x, z = (2, 6), (sub, 3 * sub), (4 * sub, 12 * sub)
    for at, (even, odd) in enumerate(zip(z + x + y, x + y + z)):
        got = lax.ppermute(mine, AXES, [(i, i ^ (odd if i % 2 else even)) for i in range(sub * dom)])
        if at < len(work) and work[at] is not None:
            zeros = work[at](mine)
            mine = (mine + got) + zeros[:1]
        else:
            mine = mine + got
    return mine, lax.ppermute(mine, "sub", twin)


def neighbour_blocks(block, sub, devices):
    pairs = [(i, i + 1) for i in range(1, devices - 1, 2)]
    other = lax.ppermute(block, AXES, pairs + [(j, i) for i, j in pairs])
    twin = lax.ppermute(block, "sub", [(i, i ^ 1) for i in range(sub)])
    return twin, other


def load_kernel(odd, tiles_hbm, x, p, tiles, gram, sems):
    parts = sems.shape[0]
    size = tiles.shape[0] // parts
    copies = [
        pltpu.make_async_copy(tiles_hbm.at[pl.ds(i * size, size)], tiles.at[pl.ds(i * size, size)], sems.at[i])
        for i in range(parts)
    ]
    for copy in copies:
        copy.start()
    both = jnp.concatenate([x[...], p[...]], 0)
    gram[...] = dot32(both, both, NT)
    for copy in copies:
        copy.wait()


def load(odd, tiles, x, p):
    cols = x.shape[0]
    vmem = pl.BlockSpec(memory_space=pltpu.VMEM)
    return pl.pallas_call(
        load_kernel,
        out_shape=(
            pltpu.VMEM(tiles.shape, tiles.dtype),
            jax.ShapeDtypeStruct((2 * cols, 2 * cols), jnp.float32),
        ),
        in_specs=[vmem, pl.BlockSpec(memory_space=pl.ANY), vmem, vmem],
        out_specs=(vmem, vmem),
        scratch_shapes=[pltpu.SemaphoreType.DMA((8,))],
        compiler_params=pltpu.CompilerParams(vmem_limit_bytes=16 * MIB),
        cost_estimate=pl.CostEstimate(flops=200000000, bytes_accessed=30000000, transcendentals=0),
    )(odd, tiles, x, p)


def fill_slabs(slabs, blocks, count, size):
    for place, block in enumerate(blocks):
        for pair in range(count // 2):
            both = block[:, pair * 2 * size : (pair + 1) * 2 * size]
            slabs[place * count + 2 * pair] = both[:, :size]
            slabs[place * count + 2 * pair + 1] = both[:, size:]


def multiply_tiles(nb, table, tiles, slabs, image, count, per):
    size = tiles.shape[2]

    def step(pair, carry):
        wide = []
        for half in range(per):
            group = pair * per + half
            total = None
            for k in range(tiles.shape[1]):
                slab = slabs[table[nb[group, k]]]
                part = lax.dot_general(tiles[group, k], slab, NT, preferred_element_type=jnp.float32)
                total = part if total is None else total + part
            wide.append(total.T)
        width = per * size
        image[:, pl.ds(pl.multiple_of(pair * width, width), width)] = jnp.concatenate(wide, 1)
        return carry

    lax.fori_loop(0, count // per, step, 0)


def first_kernel(
    per, nb, table, odd, tiles, own, twin, other, x, p, gram, x_image, p_image, mine, theirs, slabs, images
):
    count, size, cols = tiles.shape[0], tiles.shape[2], x.shape[0]
    fill_slabs(slabs, (own, twin, other), count, size)
    multiply_tiles(nb, table, tiles, slabs, images, count, per)
    image = images[:cols]
    x_image[...] = image
    p_image[...] = images[cols:]
    cross = dot16(jnp.concatenate([x[...], image, p[...]], 0), image, NT)
    g = gram[...]
    left = jnp.concatenate([g[:cols, :cols], g[cols:, :cols], g[cols:, cols:]], 0)
    split(odd, jnp.concatenate([left, cross], 1), mine, theirs)


def half_of(cols):
    return jax.ShapeDtypeStruct((3 * cols // 2, 2 * cols), jnp.float32)


def first_images(nb, table, odd, tiles, own, twin, other, x, p, gram):
    count, size, cols = tiles.shape[0], tiles.shape[2], x.shape[0]
    vmem = pl.BlockSpec(memory_space=pltpu.VMEM)
    smem = pl.BlockSpec(memory_space=pltpu.SMEM)
    return pl.pallas_call(
        functools.partial(first_kernel, 4),
        out_shape=(
            jax.ShapeDtypeStruct(x.shape, jnp.float32),
            jax.ShapeDtypeStruct(x.shape, jnp.float32),
            half_of(cols),
            half_of(cols),
        ),
        in_specs=[smem, smem] + [vmem] * 8,
        out_specs=(vmem,) * 4,
        scratch_shapes=[
            pltpu.VMEM((3 * count, 2 * cols, size), jnp.bfloat16),
            pltpu.VMEM((2 * cols, x.shape[1]), jnp.float32),
        ],
        compiler_params=pltpu.CompilerParams(vmem_limit_bytes=16 * MIB),
        cost_estimate=pl.CostEstimate(flops=10000000000, bytes_accessed=4000000, transcendentals=0),
    )(nb, table, odd, pltpu.with_memory_space_constraint(tiles, pltpu.VMEM), own, twin, other, x, p, gram)


def middle_kernel(sent, x, x_image, p, p_image, packed, zeros):
    zeros[...] = jnp.zeros_like(zeros)
    packed[...] = dot16(jnp.concatenate([x[...], x_image[...], p[...]], 0), p_image[...], NT)


def middle_products(sent, x, x_image, p, p_image):
    vmem = pl.BlockSpec(memory_space=pltpu.VMEM)
    return pl.pallas_call(
        middle_kernel,
        out_shape=(jax.ShapeDtypeStruct((3 * x.shape[0], x.shape[0]), jnp.float32), ZEROS),
        in_specs=[pl.BlockSpec(memory_space=pl.ANY)] + [vmem] * 4,
        out_specs=(vmem, vmem),
        compiler_params=pltpu.CompilerParams(vmem_limit_bytes=4 * MIB),
        cost_estimate=pl.CostEstimate(flops=1500000000, bytes_accessed=3000000, transcendentals=0),
    )(sent, x, x_image, p, p_image)


def second_kernel(
    per, nb, table, odd, tiles, own, twin, other, x, r, p, middle, quotient, parts, r_image, mine, theirs, slabs
):
    count, size = tiles.shape[0], tiles.shape[2]
    fill_slabs(slabs, (own, twin, other), count, size)
    multiply_tiles(nb, table, tiles, slabs, r_image, count, per)
    cross = dot16(jnp.concatenate([x[...], r[...], p[...]], 0), r_image[...], NT)
    c = x.shape[0]
    xp, ip, pp = middle[:c], middle[c : 2 * c], middle[2 * c :]
    rp = ip - dot32(quotient[...], xp, TN)
    split(odd, jnp.concatenate([cross, jnp.concatenate([xp, rp, pp], 0)], 1), mine, theirs)


def second_images(nb, table, odd, tiles, own, twin, other, x, r, p, middle, quotient, parts):
    count, size, cols = tiles.shape[0], tiles.shape[2], x.shape[0]
    vmem = pl.BlockSpec(memory_space=pltpu.VMEM)
    smem = pl.BlockSpec(memory_space=pltpu.SMEM)
    return pl.pallas_call(
        functools.partial(second_kernel, 4),
        out_shape=(
            jax.ShapeDtypeStruct(x.shape, jnp.float32),
            half_of(cols),
            half_of(cols),
        ),
        in_specs=[smem, smem] + [vmem] * 10 + [pl.BlockSpec(memory_space=pl.ANY)],
        out_specs=(vmem,) * 3,
        scratch_shapes=[pltpu.VMEM((3 * count, cols, size), jnp.bfloat16)],
        compiler_params=pltpu.CompilerParams(vmem_limit_bytes=16 * MIB),
        cost_estimate=pl.CostEstimate(flops=10000000000, bytes_accessed=4000000, transcendentals=0),
    )(nb, table, odd, pltpu.with_memory_space_constraint(tiles, pltpu.VMEM), own, twin, other, x, r, p, middle, quotient, parts)


def cholesky_inverse(a):
    n, step = a.shape[0], 8
    rows = lax.broadcasted_iota(jnp.int32, (step, 2 * n), 0)
    lanes = lax.broadcasted_iota(jnp.int32, (n, n), 1)
    unit = (lanes == lax.broadcasted_iota(jnp.int32, (n, n), 0)).astype(jnp.float32)
    m = jnp.concatenate([a, unit], 1)
    bands = [m[i : i + step] for i in range(0, n, step)]
    pivots = []
    for at in range(n // step):
        live = range(at, n // step)
        columns = [
            {t: jnp.broadcast_to(bands[t][:, at * step + i : at * step + i + 1], (step, 2 * n)) for t in live}
            for i in range(step)
        ]
        for i in range(step):
            pivot = columns[i][at][i : i + 1]
            pivots.append(pivot)
            over = 1.0 / pivot
            row = bands[at][i : i + 1]
            factor = {t: columns[i][t] * over for t in live}
            factor[at] = jnp.where(rows > i, factor[at], 0.0)
            for later in range(i + 1, step):
                entry = columns[later][at][i : i + 1]
                for t in live:
                    columns[later][t] = columns[later][t] - factor[t] * entry
            for t in live:
                bands[t] = bands[t] - factor[t] * row
    scale = jnp.concatenate(pivots, 0)
    return (jnp.concatenate(bands, 0) * (1.0 / jnp.sqrt(scale)))[:, n:]


def residual_kernel(odd, mine, theirs, x, x_image, packed, quotient, inverse, residual, rounded):
    cols = x.shape[0]
    packed[...] = join(odd, mine[...], theirs[...])
    gram, cross = packed[:cols, :cols], packed[:cols, cols:]
    w = cholesky_inverse(gram)
    inverse[...] = w
    q = dot32(w, dot32(w, cross, NN), TN)
    quotient[...] = q
    r = x_image[...] - dot32(q, x[...], TN)
    residual[...] = r
    rounded[...] = r.astype(jnp.bfloat16)


def residual_of(odd, mine, theirs, x, x_image):
    cols = x.shape[0]
    vmem = pl.BlockSpec(memory_space=pltpu.VMEM)
    square = jax.ShapeDtypeStruct((cols, cols), jnp.float32)
    return pl.pallas_call(
        residual_kernel,
        out_shape=(
            jax.ShapeDtypeStruct((3 * cols, 2 * cols), jnp.float32),
            square,
            square,
            jax.ShapeDtypeStruct(x.shape, jnp.float32),
            jax.ShapeDtypeStruct(x.shape, jnp.bfloat16),
        ),
        in_specs=[vmem] * 5,
        out_specs=(vmem,) * 5,
        compiler_params=pltpu.CompilerParams(vmem_limit_bytes=4 * MIB),
        cost_estimate=pl.CostEstimate(flops=3000000000, bytes_accessed=3000000, transcendentals=0),
    )(odd, mine, theirs, x, x_image)


def factor_kernel(total, packed, quotient, x_inverse, parts):
    c = quotient.shape[0]
    q = quotient[...]
    xx, px, pp = packed[:c, :c], packed[c : 2 * c, :c], packed[2 * c :, :c]
    xi, ii, pi = packed[:c, c:], packed[c : 2 * c, c:], packed[2 * c :, c:]
    rx = xi.T - dot32(q, xx, TN)
    ri = ii - dot32(q, xi, TN)
    rr = ri - dot32(rx, q, NN)
    pr = pi - dot32(px, q, NN)
    scale = 1.0 / total
    w1 = x_inverse[...] * (total**0.5)
    l21, l31 = dot32(rx * scale, w1, NT), dot32(px * scale, w1, NT)
    w2 = cholesky_inverse(rr * scale - dot32(l21, l21, NT))
    l32 = dot32(pr * scale - dot32(l31, l21, NT), w2, NT)
    last = pp * scale - dot32(l31, l31, NT) - dot32(l32, l32, NT)
    for at, part in enumerate((w1, w2, l21, l31, l32, last, ri)):
        parts[at] = part


def factor(total, packed, quotient, x_inverse):
    c = quotient.shape[0]
    vmem = pl.BlockSpec(memory_space=pltpu.VMEM)
    return pl.pallas_call(
        functools.partial(factor_kernel, total),
        out_shape=jax.ShapeDtypeStruct((7, c, c), jnp.float32),
        in_specs=[vmem] * 3,
        out_specs=vmem,
        compiler_params=pltpu.CompilerParams(vmem_limit_bytes=4 * MIB),
        cost_estimate=pl.CostEstimate(flops=2000000000, bytes_accessed=3000000, transcendentals=0),
    )(packed, quotient, x_inverse)


def inverse_kernel(sent, parts, inverse, zeros):
    zeros[...] = jnp.zeros_like(zeros)
    w1, w2, l21, l31, l32 = parts[0], parts[1], parts[2], parts[3], parts[4]
    w21 = -dot32(w2, dot32(l21, w1, NN), NN)
    below = dot32(l31, w1, NN) + dot32(l32, w21, NN)
    beside = dot32(l32, w2, NN)
    w3 = cholesky_inverse(parts[5])
    w3_below = -dot32(w3, jnp.concatenate([below, beside], 1), NN)
    zero = jnp.zeros_like(w1)
    inverse[...] = jnp.concatenate(
        [
            jnp.concatenate([w1, zero, zero], 1),
            jnp.concatenate([w21, w2, zero], 1),
            jnp.concatenate([w3_below, w3], 1),
        ],
        0,
    )


def inverse_of(sent, parts):
    width = 3 * parts.shape[1]
    vmem = pl.BlockSpec(memory_space=pltpu.VMEM)
    return pl.pallas_call(
        inverse_kernel,
        out_shape=(jax.ShapeDtypeStruct((width, width), jnp.float32), ZEROS),
        in_specs=[pl.BlockSpec(memory_space=pl.ANY), vmem],
        out_specs=(vmem, vmem),
        compiler_params=pltpu.CompilerParams(vmem_limit_bytes=4 * MIB),
        cost_estimate=pl.CostEstimate(flops=2000000000, bytes_accessed=3000000, transcendentals=0),
    )(sent, parts)


def basis_kernel(extra, sent, inverse, x, r, p, x_image, r_image, p_image, *rest):
    basis, basis_image, zeros = rest[extra:]
    zeros[...] = jnp.zeros_like(zeros)
    w = inverse[...]
    basis[...] = dot16(w, jnp.concatenate([x[...], r[...], p[...]], 0), NN)
    basis_image[...] = dot16(w, jnp.concatenate([x_image[...], r_image[...], p_image[...]], 0), NN)


def bases(part, parts, sent, inverse, blocks, done):
    width, rows = inverse.shape[0], blocks[0].shape[1]
    cols = blocks[0].shape[0]
    tile = 768
    steps = rows // tile // parts
    first = part * steps
    whole = pl.BlockSpec(memory_space=pl.ANY)
    block = pl.BlockSpec((cols, tile), lambda i: (0, first + i))
    out = pl.BlockSpec((width, tile), lambda i: (0, first + i))
    return pl.pallas_call(
        functools.partial(basis_kernel, len(done)),
        grid=(steps,),
        out_shape=(jax.ShapeDtypeStruct((width, rows), jnp.float32),) * 2 + (ZEROS,),
        in_specs=[whole, pl.BlockSpec((width, width), lambda i: (0, 0))] + [block] * 6 + [whole] * len(done),
        out_specs=(out, out, pl.BlockSpec((8, 128), lambda i: (0, 0))),
        input_output_aliases={8 + i: i for i in range(len(done))},
        compiler_params=pltpu.CompilerParams(vmem_limit_bytes=12 * MIB),
        cost_estimate=pl.CostEstimate(flops=2000000000, bytes_accessed=3000000, transcendentals=0),
    )(sent, inverse, *blocks, *done)


def project_kernel(total, odd, inverse, packed, parts, mine, theirs, projected):
    c = parts.shape[1]
    left = jnp.concatenate([packed[:c, c:], parts[6], packed[2 * c :, c:]], 0)
    w = inverse[...]
    cross = jnp.concatenate([left, join(odd, mine[...], theirs[...])], 1)
    projected[...] = dot16(dot16(w, cross, NN), w, NT) * (1.0 / total)


def project(total, odd, inverse, packed, parts, mine, theirs):
    vmem = pl.BlockSpec(memory_space=pltpu.VMEM)
    return pl.pallas_call(
        functools.partial(project_kernel, total),
        out_shape=jax.ShapeDtypeStruct(inverse.shape, jnp.float32),
        in_specs=[vmem] * 6,
        out_specs=vmem,
        compiler_params=pltpu.CompilerParams(vmem_limit_bytes=16 * MIB),
    )(odd, inverse, packed, parts, mine, theirs)


def shards(sub, dom, tile_blocks, neighbours, send_groups, block_x, block_p):
    devices = sub * dom
    count, rows, cols = tile_blocks.shape[0], block_x.shape[0], block_x.shape[1]
    total = float(rows * devices)
    x, p = block_x.T, block_p.T
    lists = jnp.pad(send_groups.astype(jnp.bfloat16)[None], ((0, 2 * cols - 1), (0, 128 - 2 * count)))
    both = jnp.concatenate([jnp.concatenate([x, p], 0).astype(jnp.bfloat16), lists], 1)
    odd = jnp.broadcast_to(lax.axis_index("sub") % 2, (8, 2 * cols)).astype(jnp.float32)
    twin, other = neighbour_blocks(both, sub, devices)
    twin_list = twin[0, rows : rows + 2 * count].astype(jnp.int32) + count
    other_list = other[0, rows : rows + 2 * count].astype(jnp.int32) + 2 * count
    first_half = odd[0, :count] > 0
    table = jnp.concatenate(
        [
            jnp.where(first_half, twin_list[count:], other_list[count:]),
            jnp.arange(count, dtype=jnp.int32),
            jnp.where(first_half, other_list[:count], twin_list[:count]),
        ]
    )
    tiles, gram = load(odd, tile_blocks, x, p)
    x_image, p_image, *halves = first_images(neighbours, table, odd, tiles, both, twin, other, x, p, gram)
    made = {}

    def step(name, make):
        def run(sent):
            *values, zeros = make(sent)
            made[name] = values
            return zeros

        return run

    halves = all_sum(
        *halves, sub, dom, [step("middle", lambda sent: middle_products(sent, x, x_image, p, p_image))]
    )
    packed, quotient, x_inverse, residual, r_round = residual_of(odd, *halves, x, x_image)
    r_twin, r_other = neighbour_blocks(r_round, sub, devices)
    parts = factor(total, packed, quotient, x_inverse)
    r_image, *halves = second_images(
        neighbours, table, odd, tiles, r_round, r_twin, r_other, x, residual, p, made["middle"][0], quotient, parts
    )
    blocks = (x, residual, p, x_image, r_image, p_image)
    made["bases"] = []
    pieces = 4
    work = [
        step("inverse", lambda sent: inverse_of(sent, parts)),
    ]
    for piece in range(pieces):
        work.append(
            step(
                "bases",
                lambda sent, piece=piece: bases(piece, pieces, sent, made["inverse"][0], blocks, made["bases"]),
            )
        )
    halves = all_sum(*halves, sub, dom, work)
    basis, basis_image = made["bases"]
    projected = project(total, odd, made["inverse"][0], packed, parts, *halves)
    return basis.T, basis_image.T, projected


def solution(mesh):
    placed = (
        P(AXES, None, None, None),
        P(AXES, None),
        P(AXES),
        P(AXES, None),
        P(AXES, None),
    )
    return jax.shard_map(
        functools.partial(shards, mesh.shape["sub"], mesh.shape["dom"]),
        mesh=mesh,
        in_specs=placed,
        out_specs=(P(AXES, None), P(AXES, None), P()),
        check_vma=False,
    )
```

```python
import functools

import jax
import jax.numpy as jnp
from jax import lax
from jax.experimental import pallas as pl
from jax.experimental.pallas import tpu as pltpu
from jax.sharding import PartitionSpec as P

AXES = ("dom", "sub")
HIGHEST = lax.Precision.HIGHEST
MIB = 2**20
PER = 8
NT = (((1,), (1,)), ((), ()))
TN = (((0,), (0,)), ((), ()))
NN = (((1,), (0,)), ((), ()))
ZEROS = jax.ShapeDtypeStruct((8, 128), jnp.float32)


def dot32(a, b, dims):
    return lax.dot_general(a, b, dims, precision=HIGHEST, preferred_element_type=jnp.float32)


def halves_of(a):
    high = a.astype(jnp.bfloat16)
    return high, (a - high.astype(jnp.float32)).astype(jnp.bfloat16)


def dot16(a, b, dims):
    (a_high, a_low), (b_high, b_low) = halves_of(a), halves_of(b)
    dot = functools.partial(lax.dot_general, dimension_numbers=dims, preferred_element_type=jnp.float32)
    return dot(a_high, b_high) + (dot(a_high, b_low) + dot(a_low, b_high))


def split(odd, value, mine, theirs):
    half = value.shape[0] // 2
    mine[...] = jnp.where(odd[:1] > 0, value[half:], value[:half])
    theirs[...] = jnp.where(odd[:1] > 0, value[:half], value[half:])


def join(odd, mine, theirs):
    first = jnp.where(odd[:1] > 0, theirs, mine)
    second = jnp.where(odd[:1] > 0, mine, theirs)
    return jnp.concatenate([first, second], 0)


def all_sum(mine, theirs, sub, dom, work=()):
    twin = [(i, i ^ 1) for i in range(sub)]
    mine = mine + lax.ppermute(theirs, "sub", twin)
    y, x, z = (2, 6), (sub, 3 * sub), (4 * sub, 12 * sub)
    for at, (even, odd) in enumerate(zip(z + x + y, x + y + z)):
        got = lax.ppermute(mine, AXES, [(i, i ^ (odd if i % 2 else even)) for i in range(sub * dom)])
        if at < len(work) and work[at] is not None:
            zeros = work[at](mine)
            mine = (mine + got) + zeros[:1]
        else:
            mine = mine + got
    return mine, lax.ppermute(mine, "sub", twin)


def neighbour_blocks(block, sub, devices):
    pairs = [(i, i + 1) for i in range(1, devices - 1, 2)]
    other = lax.ppermute(block, AXES, pairs + [(j, i) for i, j in pairs])
    twin = lax.ppermute(block, "sub", [(i, i ^ 1) for i in range(sub)])
    return twin, other


def load_kernel(odd, tiles_hbm, x, p, packed, gram, arrived, sems):
    count, degree, _, size = tiles_hbm.shape
    depth = arrived.shape[0]

    def copy(group, slot):
        return pltpu.make_async_copy(tiles_hbm.at[group], arrived.at[slot], sems.at[slot])

    for slot in range(depth):
        copy(slot, slot).start()
    both = jnp.concatenate([x[...], p[...]], 0)
    gram[...] = dot32(both, both, NT)

    def step(group, carry):
        slot = lax.rem(group, depth)
        copy(group, slot).wait()
        for pair in range(degree // 2):
            packed[group, :, 2 * pair * size : 2 * (pair + 1) * size] = jnp.concatenate(
                [arrived[slot, 2 * pair], arrived[slot, 2 * pair + 1]], 1
            )

        @pl.when(group + depth < count)
        def _():
            copy(group + depth, slot).start()

        return carry

    lax.fori_loop(0, count, step, 0)


def load(odd, tiles, x, p):
    cols = x.shape[0]
    count, degree, size = tiles.shape[:3]
    depth = 4
    vmem = pl.BlockSpec(memory_space=pltpu.VMEM)
    return pl.pallas_call(
        load_kernel,
        out_shape=(
            pltpu.VMEM((count, size, degree * size), tiles.dtype),
            jax.ShapeDtypeStruct((2 * cols, 2 * cols), jnp.float32),
        ),
        in_specs=[vmem, pl.BlockSpec(memory_space=pl.ANY), vmem, vmem],
        out_specs=(vmem, vmem),
        scratch_shapes=[
            pltpu.VMEM((depth,) + tiles.shape[1:], tiles.dtype),
            pltpu.SemaphoreType.DMA((depth,)),
        ],
        compiler_params=pltpu.CompilerParams(vmem_limit_bytes=20 * MIB),
        cost_estimate=pl.CostEstimate(flops=200000000, bytes_accessed=30000000, transcendentals=0),
    )(odd, tiles, x, p)


def fill_slabs(low, high, blocks, count, size):
    cols, lanes = low.shape[1:]
    gap = jnp.zeros((cols, lanes - size), low.dtype)
    for place, block in enumerate(blocks):
        for pair in range(count // 2):
            both = block[:, pair * 2 * size : (pair + 1) * 2 * size]
            for half, slab in enumerate((both[:, :size], both[:, size:])):
                low[place * count + 2 * pair + half] = jnp.concatenate([slab, gap], 1)
                high[place * count + 2 * pair + half] = jnp.concatenate([gap, slab], 1)


def multiply_tiles(nb, table, tiles, low, high, ends, image):
    count, size, depth = tiles.shape
    per, lanes = ends.shape[0], low.shape[2]
    rest = 2 * size - lanes

    def step(turn, carry):
        wide = []
        for part in range(per):
            group = turn * per + part
            for pair in range(depth // (2 * size)):
                first = low[table[nb[group, 2 * pair]]]
                second = high[table[nb[group, 2 * pair + 1]]]
                at = 2 * pair * size
                ends[part, :, at : at + rest] = first[:, :rest]
                ends[part, :, at + rest : at + lanes] = first[:, rest:] + second[:, : lanes - rest]
                ends[part, :, at + lanes : at + 2 * size] = second[:, lanes - rest :]
            total = lax.dot_general(tiles[group], ends[part], NT, preferred_element_type=jnp.float32)
            wide.append(total.T)
        width = per * size
        image[:, pl.ds(pl.multiple_of(turn * width, width), width)] = jnp.concatenate(wide, 1)
        return carry

    lax.fori_loop(0, count // per, step, 0)


def slab_scratch(count, cols, size, depth, per):
    lanes = -(-size // 128) * 128
    slabs = pltpu.VMEM((3 * count, cols, lanes), jnp.bfloat16)
    return [slabs, slabs, pltpu.VMEM((per, cols, depth), jnp.bfloat16)]


def first_kernel(
    nb, table, odd, tiles, own, twin, other, x, p, gram, x_image, p_image, mine, theirs, low, high, ends, images
):
    count, size, cols = tiles.shape[0], tiles.shape[1], x.shape[0]
    fill_slabs(low, high, (own, twin, other), count, size)
    multiply_tiles(nb, table, tiles, low, high, ends, images)
    image = images[:cols]
    x_image[...] = image
    p_image[...] = images[cols:]
    cross = dot16(jnp.concatenate([x[...], image, p[...]], 0), image, NT)
    g = gram[...]
    left = jnp.concatenate([g[:cols, :cols], g[cols:, :cols], g[cols:, cols:]], 0)
    split(odd, jnp.concatenate([left, cross], 1), mine, theirs)


def half_of(cols):
    return jax.ShapeDtypeStruct((3 * cols // 2, 2 * cols), jnp.float32)


def first_images(nb, table, odd, tiles, own, twin, other, x, p, gram):
    (count, size, depth), cols = tiles.shape, x.shape[0]
    vmem = pl.BlockSpec(memory_space=pltpu.VMEM)
    smem = pl.BlockSpec(memory_space=pltpu.SMEM)
    return pl.pallas_call(
        first_kernel,
        out_shape=(
            jax.ShapeDtypeStruct(x.shape, jnp.float32),
            jax.ShapeDtypeStruct(x.shape, jnp.float32),
            half_of(cols),
            half_of(cols),
        ),
        in_specs=[smem, smem] + [vmem] * 8,
        out_specs=(vmem,) * 4,
        scratch_shapes=[
            *slab_scratch(count, 2 * cols, size, depth, PER),
            pltpu.VMEM((2 * cols, x.shape[1]), jnp.float32),
        ],
        compiler_params=pltpu.CompilerParams(vmem_limit_bytes=20 * MIB),
        cost_estimate=pl.CostEstimate(flops=10000000000, bytes_accessed=4000000, transcendentals=0),
    )(nb, table, odd, pltpu.with_memory_space_constraint(tiles, pltpu.VMEM), own, twin, other, x, p, gram)


def middle_kernel(sent, x, x_image, p, p_image, packed, zeros):
    zeros[...] = jnp.zeros_like(zeros)
    packed[...] = dot16(jnp.concatenate([x[...], x_image[...], p[...]], 0), p_image[...], NT)


def middle_products(sent, x, x_image, p, p_image):
    vmem = pl.BlockSpec(memory_space=pltpu.VMEM)
    return pl.pallas_call(
        middle_kernel,
        out_shape=(jax.ShapeDtypeStruct((3 * x.shape[0], x.shape[0]), jnp.float32), ZEROS),
        in_specs=[pl.BlockSpec(memory_space=pl.ANY)] + [vmem] * 4,
        out_specs=(vmem, vmem),
        compiler_params=pltpu.CompilerParams(vmem_limit_bytes=4 * MIB),
        cost_estimate=pl.CostEstimate(flops=1500000000, bytes_accessed=3000000, transcendentals=0),
    )(sent, x, x_image, p, p_image)


def second_kernel(
    nb, table, odd, tiles, own, twin, other, x, r, p, middle, quotient, parts, r_image, mine, theirs, low, high, ends
):
    count, size = tiles.shape[0], tiles.shape[1]
    fill_slabs(low, high, (own, twin, other), count, size)
    multiply_tiles(nb, table, tiles, low, high, ends, r_image)
    cross = dot16(jnp.concatenate([x[...], r[...], p[...]], 0), r_image[...], NT)
    c = x.shape[0]
    xp, ip, pp = middle[:c], middle[c : 2 * c], middle[2 * c :]
    rp = ip - dot32(quotient[...], xp, TN)
    split(odd, jnp.concatenate([cross, jnp.concatenate([xp, rp, pp], 0)], 1), mine, theirs)


def second_images(nb, table, odd, tiles, own, twin, other, x, r, p, middle, quotient, parts):
    (count, size, depth), cols = tiles.shape, x.shape[0]
    vmem = pl.BlockSpec(memory_space=pltpu.VMEM)
    smem = pl.BlockSpec(memory_space=pltpu.SMEM)
    return pl.pallas_call(
        second_kernel,
        out_shape=(
            jax.ShapeDtypeStruct(x.shape, jnp.float32),
            half_of(cols),
            half_of(cols),
        ),
        in_specs=[smem, smem] + [vmem] * 10 + [pl.BlockSpec(memory_space=pl.ANY)],
        out_specs=(vmem,) * 3,
        scratch_shapes=slab_scratch(count, cols, size, depth, PER),
        compiler_params=pltpu.CompilerParams(vmem_limit_bytes=20 * MIB),
        cost_estimate=pl.CostEstimate(flops=10000000000, bytes_accessed=4000000, transcendentals=0),
    )(nb, table, odd, pltpu.with_memory_space_constraint(tiles, pltpu.VMEM), own, twin, other, x, r, p, middle, quotient, parts)


def cholesky_inverse(a):
    n, step = a.shape[0], 8
    rows = lax.broadcasted_iota(jnp.int32, (step, 2 * n), 0)
    lanes = lax.broadcasted_iota(jnp.int32, (n, n), 1)
    unit = (lanes == lax.broadcasted_iota(jnp.int32, (n, n), 0)).astype(jnp.float32)
    m = jnp.concatenate([a, unit], 1)
    bands = [m[i : i + step] for i in range(0, n, step)]
    pivots = []
    for at in range(n // step):
        live = range(at, n // step)
        columns = [
            {t: jnp.broadcast_to(bands[t][:, at * step + i : at * step + i + 1], (step, 2 * n)) for t in live}
            for i in range(step)
        ]
        for i in range(step):
            pivot = columns[i][at][i : i + 1]
            pivots.append(pivot)
            over = 1.0 / pivot
            row = bands[at][i : i + 1]
            factor = {t: columns[i][t] * over for t in live}
            factor[at] = jnp.where(rows > i, factor[at], 0.0)
            for later in range(i + 1, step):
                entry = columns[later][at][i : i + 1]
                for t in live:
                    columns[later][t] = columns[later][t] - factor[t] * entry
            for t in live:
                bands[t] = bands[t] - factor[t] * row
    scale = jnp.concatenate(pivots, 0)
    return (jnp.concatenate(bands, 0) * (1.0 / jnp.sqrt(scale)))[:, n:]


def residual_kernel(odd, mine, theirs, x, x_image, packed, quotient, inverse, residual, rounded):
    cols = x.shape[0]
    packed[...] = join(odd, mine[...], theirs[...])
    gram, cross = packed[:cols, :cols], packed[:cols, cols:]
    w = cholesky_inverse(gram)
    inverse[...] = w
    q = dot32(w, dot32(w, cross, NN), TN)
    quotient[...] = q
    r = x_image[...] - dot32(q, x[...], TN)
    residual[...] = r
    rounded[...] = r.astype(jnp.bfloat16)


def residual_of(odd, mine, theirs, x, x_image):
    cols = x.shape[0]
    vmem = pl.BlockSpec(memory_space=pltpu.VMEM)
    square = jax.ShapeDtypeStruct((cols, cols), jnp.float32)
    return pl.pallas_call(
        residual_kernel,
        out_shape=(
            jax.ShapeDtypeStruct((3 * cols, 2 * cols), jnp.float32),
            square,
            square,
            jax.ShapeDtypeStruct(x.shape, jnp.float32),
            jax.ShapeDtypeStruct(x.shape, jnp.bfloat16),
        ),
        in_specs=[vmem] * 5,
        out_specs=(vmem,) * 5,
        compiler_params=pltpu.CompilerParams(vmem_limit_bytes=4 * MIB),
        cost_estimate=pl.CostEstimate(flops=3000000000, bytes_accessed=3000000, transcendentals=0),
    )(odd, mine, theirs, x, x_image)


def factor_kernel(total, packed, quotient, x_inverse, parts):
    c = quotient.shape[0]
    q = quotient[...]
    xx, px, pp = packed[:c, :c], packed[c : 2 * c, :c], packed[2 * c :, :c]
    xi, ii, pi = packed[:c, c:], packed[c : 2 * c, c:], packed[2 * c :, c:]
    rx = xi.T - dot32(q, xx, TN)
    ri = ii - dot32(q, xi, TN)
    rr = ri - dot32(rx, q, NN)
    pr = pi - dot32(px, q, NN)
    scale = 1.0 / total
    w1 = x_inverse[...] * (total**0.5)
    l21, l31 = dot32(rx * scale, w1, NT), dot32(px * scale, w1, NT)
    w2 = cholesky_inverse(rr * scale - dot32(l21, l21, NT))
    l32 = dot32(pr * scale - dot32(l31, l21, NT), w2, NT)
    last = pp * scale - dot32(l31, l31, NT) - dot32(l32, l32, NT)
    for at, part in enumerate((w1, w2, l21, l31, l32, last, ri)):
        parts[at] = part


def factor(total, packed, quotient, x_inverse):
    c = quotient.shape[0]
    vmem = pl.BlockSpec(memory_space=pltpu.VMEM)
    return pl.pallas_call(
        functools.partial(factor_kernel, total),
        out_shape=jax.ShapeDtypeStruct((7, c, c), jnp.float32),
        in_specs=[vmem] * 3,
        out_specs=vmem,
        compiler_params=pltpu.CompilerParams(vmem_limit_bytes=4 * MIB),
        cost_estimate=pl.CostEstimate(flops=2000000000, bytes_accessed=3000000, transcendentals=0),
    )(packed, quotient, x_inverse)


def inverse_kernel(sent, parts, inverse, zeros):
    zeros[...] = jnp.zeros_like(zeros)
    w1, w2, l21, l31, l32 = parts[0], parts[1], parts[2], parts[3], parts[4]
    w21 = -dot32(w2, dot32(l21, w1, NN), NN)
    below = dot32(l31, w1, NN) + dot32(l32, w21, NN)
    beside = dot32(l32, w2, NN)
    w3 = cholesky_inverse(parts[5])
    w3_below = -dot32(w3, jnp.concatenate([below, beside], 1), NN)
    zero = jnp.zeros_like(w1)
    inverse[...] = jnp.concatenate(
        [
            jnp.concatenate([w1, zero, zero], 1),
            jnp.concatenate([w21, w2, zero], 1),
            jnp.concatenate([w3_below, w3], 1),
        ],
        0,
    )


def inverse_of(sent, parts):
    width = 3 * parts.shape[1]
    vmem = pl.BlockSpec(memory_space=pltpu.VMEM)
    return pl.pallas_call(
        inverse_kernel,
        out_shape=(jax.ShapeDtypeStruct((width, width), jnp.float32), ZEROS),
        in_specs=[pl.BlockSpec(memory_space=pl.ANY), vmem],
        out_specs=(vmem, vmem),
        compiler_params=pltpu.CompilerParams(vmem_limit_bytes=4 * MIB),
        cost_estimate=pl.CostEstimate(flops=2000000000, bytes_accessed=3000000, transcendentals=0),
    )(sent, parts)


def basis_kernel(extra, sent, inverse, x, r, p, x_image, r_image, p_image, *rest):
    basis, basis_image, zeros = rest[extra:]
    zeros[...] = jnp.zeros_like(zeros)
    w = inverse[...]
    basis[...] = dot16(w, jnp.concatenate([x[...], r[...], p[...]], 0), NN)
    basis_image[...] = dot16(w, jnp.concatenate([x_image[...], r_image[...], p_image[...]], 0), NN)


def bases(part, parts, sent, inverse, blocks, done):
    width, rows = inverse.shape[0], blocks[0].shape[1]
    cols = blocks[0].shape[0]
    tile = 768
    steps = rows // tile // parts
    first = part * steps
    whole = pl.BlockSpec(memory_space=pl.ANY)
    block = pl.BlockSpec((cols, tile), lambda i: (0, first + i))
    out = pl.BlockSpec((width, tile), lambda i: (0, first + i))
    return pl.pallas_call(
        functools.partial(basis_kernel, len(done)),
        grid=(steps,),
        out_shape=(jax.ShapeDtypeStruct((width, rows), jnp.float32),) * 2 + (ZEROS,),
        in_specs=[whole, pl.BlockSpec((width, width), lambda i: (0, 0))] + [block] * 6 + [whole] * len(done),
        out_specs=(out, out, pl.BlockSpec((8, 128), lambda i: (0, 0))),
        input_output_aliases={8 + i: i for i in range(len(done))},
        compiler_params=pltpu.CompilerParams(vmem_limit_bytes=12 * MIB),
        cost_estimate=pl.CostEstimate(flops=2000000000, bytes_accessed=3000000, transcendentals=0),
    )(sent, inverse, *blocks, *done)


def project_kernel(total, odd, inverse, packed, parts, mine, theirs, projected):
    c = parts.shape[1]
    left = jnp.concatenate([packed[:c, c:], parts[6], packed[2 * c :, c:]], 0)
    w = inverse[...]
    cross = jnp.concatenate([left, join(odd, mine[...], theirs[...])], 1)
    projected[...] = dot16(dot16(w, cross, NN), w, NT) * (1.0 / total)


def project(total, odd, inverse, packed, parts, mine, theirs):
    vmem = pl.BlockSpec(memory_space=pltpu.VMEM)
    return pl.pallas_call(
        functools.partial(project_kernel, total),
        out_shape=jax.ShapeDtypeStruct(inverse.shape, jnp.float32),
        in_specs=[vmem] * 6,
        out_specs=vmem,
        compiler_params=pltpu.CompilerParams(vmem_limit_bytes=20 * MIB),
    )(odd, inverse, packed, parts, mine, theirs)


def shards(sub, dom, tile_blocks, neighbours, send_groups, block_x, block_p):
    devices = sub * dom
    count, rows, cols = tile_blocks.shape[0], block_x.shape[0], block_x.shape[1]
    total = float(rows * devices)
    x, p = block_x.T, block_p.T
    lists = jnp.pad(send_groups.astype(jnp.bfloat16)[None], ((0, 2 * cols - 1), (0, 128 - 2 * count)))
    both = jnp.concatenate([jnp.concatenate([x, p], 0).astype(jnp.bfloat16), lists], 1)
    odd = jnp.broadcast_to(lax.axis_index("sub") % 2, (8, 2 * cols)).astype(jnp.float32)
    twin, other = neighbour_blocks(both, sub, devices)
    twin_list = twin[0, rows : rows + 2 * count].astype(jnp.int32) + count
    other_list = other[0, rows : rows + 2 * count].astype(jnp.int32) + 2 * count
    first_half = odd[0, :count] > 0
    table = jnp.concatenate(
        [
            jnp.where(first_half, twin_list[count:], other_list[count:]),
            jnp.arange(count, dtype=jnp.int32),
            jnp.where(first_half, other_list[:count], twin_list[:count]),
        ]
    )
    tiles, gram = load(odd, tile_blocks, x, p)
    x_image, p_image, *halves = first_images(neighbours, table, odd, tiles, both, twin, other, x, p, gram)
    made = {}

    def step(name, make):
        def run(sent):
            *values, zeros = make(sent)
            made[name] = values
            return zeros

        return run

    halves = all_sum(
        *halves, sub, dom, [step("middle", lambda sent: middle_products(sent, x, x_image, p, p_image))]
    )
    packed, quotient, x_inverse, residual, r_round = residual_of(odd, *halves, x, x_image)
    r_twin, r_other = neighbour_blocks(r_round, sub, devices)
    parts = factor(total, packed, quotient, x_inverse)
    r_image, *halves = second_images(
        neighbours, table, odd, tiles, r_round, r_twin, r_other, x, residual, p, made["middle"][0], quotient, parts
    )
    blocks = (x, residual, p, x_image, r_image, p_image)
    made["bases"] = []
    pieces = 4
    work = [
        step("inverse", lambda sent: inverse_of(sent, parts)),
    ]
    for piece in range(pieces):
        work.append(
            step(
                "bases",
                lambda sent, piece=piece: bases(piece, pieces, sent, made["inverse"][0], blocks, made["bases"]),
            )
        )
    halves = all_sum(*halves, sub, dom, work)
    basis, basis_image = made["bases"]
    projected = project(total, odd, made["inverse"][0], packed, parts, *halves)
    return basis.T, basis_image.T, projected


def solution(mesh):
    placed = (
        P(AXES, None, None, None),
        P(AXES, None),
        P(AXES),
        P(AXES, None),
        P(AXES, None),
    )
    return jax.shard_map(
        functools.partial(shards, mesh.shape["sub"], mesh.shape["dom"]),
        mesh=mesh,
        in_specs=placed,
        out_specs=(P(AXES, None), P(AXES, None), P()),
        check_vma=False,
    )
```

```python
import functools

import jax
import jax.numpy as jnp
from jax import lax
from jax.experimental import pallas as pl
from jax.experimental.pallas import tpu as pltpu
from jax.sharding import PartitionSpec as P

AXES = ("dom", "sub")
HIGHEST = lax.Precision.HIGHEST
MIB = 2**20
PER = 8
NT = (((1,), (1,)), ((), ()))
TN = (((0,), (0,)), ((), ()))
NN = (((1,), (0,)), ((), ()))
ZEROS = jax.ShapeDtypeStruct((8, 128), jnp.float32)


def dot32(a, b, dims):
    return lax.dot_general(a, b, dims, precision=HIGHEST, preferred_element_type=jnp.float32)


def halves_of(a):
    high = a.astype(jnp.bfloat16)
    return high, (a - high.astype(jnp.float32)).astype(jnp.bfloat16)


def dot16(a, b, dims):
    (a_high, a_low), (b_high, b_low) = halves_of(a), halves_of(b)
    dot = functools.partial(lax.dot_general, dimension_numbers=dims, preferred_element_type=jnp.float32)
    return dot(a_high, b_high) + (dot(a_high, b_low) + dot(a_low, b_high))


def split(odd, value, mine, theirs):
    half = value.shape[0] // 2
    mine[...] = jnp.where(odd[:1] > 0, value[half:], value[:half])
    theirs[...] = jnp.where(odd[:1] > 0, value[:half], value[half:])


def join(odd, mine, theirs):
    first = jnp.where(odd[:1] > 0, theirs, mine)
    second = jnp.where(odd[:1] > 0, mine, theirs)
    return jnp.concatenate([first, second], 0)


def all_sum(mine, theirs, sub, dom, work=()):
    twin = [(i, i ^ 1) for i in range(sub)]
    mine = mine + lax.ppermute(theirs, "sub", twin)
    y, x, z = (2, 6), (sub, 3 * sub), (4 * sub, 12 * sub)
    for at, (even, odd) in enumerate(zip(z + x + y, x + z + y)):
        got = lax.ppermute(mine, AXES, [(i, i ^ (odd if i % 2 else even)) for i in range(sub * dom)])
        if at < len(work) and work[at] is not None:
            zeros = work[at](mine)
            mine = (mine + got) + zeros[:1]
        else:
            mine = mine + got
    return mine, lax.ppermute(mine, "sub", twin)


def neighbour_blocks(block, sub, devices):
    pairs = [(i, i + 1) for i in range(1, devices - 1, 2)]
    other = lax.ppermute(block, AXES, pairs + [(j, i) for i, j in pairs])
    twin = lax.ppermute(block, "sub", [(i, i ^ 1) for i in range(sub)])
    return twin, other


def load_kernel(odd, tiles_hbm, x, p, packed, gram, arrived, sems):
    count, degree, _, size = tiles_hbm.shape
    depth = arrived.shape[0]

    def copy(group, slot):
        return pltpu.make_async_copy(tiles_hbm.at[group], arrived.at[slot], sems.at[slot])

    for slot in range(depth):
        copy(slot, slot).start()
    both = jnp.concatenate([x[...], p[...]], 0)
    gram[...] = dot16(both, both, NT)

    def step(group, carry):
        slot = lax.rem(group, depth)
        copy(group, slot).wait()
        for pair in range(degree // 2):
            packed[group, :, 2 * pair * size : 2 * (pair + 1) * size] = jnp.concatenate(
                [arrived[slot, 2 * pair], arrived[slot, 2 * pair + 1]], 1
            )

        @pl.when(group + depth < count)
        def _():
            copy(group + depth, slot).start()

        return carry

    lax.fori_loop(0, count, step, 0)


def load(odd, tiles, x, p):
    cols = x.shape[0]
    count, degree, size = tiles.shape[:3]
    depth = 4
    vmem = pl.BlockSpec(memory_space=pltpu.VMEM)
    return pl.pallas_call(
        load_kernel,
        out_shape=(
            pltpu.VMEM((count, size, degree * size), tiles.dtype),
            jax.ShapeDtypeStruct((2 * cols, 2 * cols), jnp.float32),
        ),
        in_specs=[vmem, pl.BlockSpec(memory_space=pl.ANY), vmem, vmem],
        out_specs=(vmem, vmem),
        scratch_shapes=[
            pltpu.VMEM((depth,) + tiles.shape[1:], tiles.dtype),
            pltpu.SemaphoreType.DMA((depth,)),
        ],
        compiler_params=pltpu.CompilerParams(vmem_limit_bytes=20 * MIB),
        cost_estimate=pl.CostEstimate(flops=200000000, bytes_accessed=30000000, transcendentals=0),
    )(odd, tiles, x, p)


def fill_slabs(low, high, blocks, count, size):
    cols, lanes = low.shape[1:]
    gap = jnp.zeros((cols, lanes - size), low.dtype)
    for place, block in enumerate(blocks):
        for pair in range(count // 2):
            both = block[:, pair * 2 * size : (pair + 1) * 2 * size]
            for half, slab in enumerate((both[:, :size], both[:, size:])):
                low[place * count + 2 * pair + half] = jnp.concatenate([slab, gap], 1)
                high[place * count + 2 * pair + half] = jnp.concatenate([gap, slab], 1)


def multiply_tiles(nb, table, tiles, low, high, ends, image):
    count, size, depth = tiles.shape
    per, lanes = ends.shape[0], low.shape[2]
    rest = 2 * size - lanes

    def step(turn, carry):
        wide = []
        for part in range(per):
            group = turn * per + part
            for pair in range(depth // (2 * size)):
                first = low[table[nb[group, 2 * pair]]]
                second = high[table[nb[group, 2 * pair + 1]]]
                at = 2 * pair * size
                ends[part, :, at : at + rest] = first[:, :rest]
                ends[part, :, at + rest : at + lanes] = first[:, rest:] + second[:, : lanes - rest]
                ends[part, :, at + lanes : at + 2 * size] = second[:, lanes - rest :]
            total = lax.dot_general(tiles[group], ends[part], NT, preferred_element_type=jnp.float32)
            wide.append(total.T)
        width = per * size
        image[:, pl.ds(pl.multiple_of(turn * width, width), width)] = jnp.concatenate(wide, 1)
        return carry

    lax.fori_loop(0, count // per, step, 0)


def slab_scratch(count, cols, size, depth, per):
    lanes = -(-size // 128) * 128
    slabs = pltpu.VMEM((3 * count, cols, lanes), jnp.bfloat16)
    return [slabs, slabs, pltpu.VMEM((per, cols, depth), jnp.bfloat16)]


def first_kernel(
    nb, table, odd, tiles, own, twin, other, x, p, gram, x_image, p_image, mine, theirs, low, high, ends, images
):
    count, size, cols = tiles.shape[0], tiles.shape[1], x.shape[0]
    fill_slabs(low, high, (own, twin, other), count, size)
    multiply_tiles(nb, table, tiles, low, high, ends, images)
    image = images[:cols]
    x_image[...] = image
    p_image[...] = images[cols:]
    cross = dot16(jnp.concatenate([x[...], image, p[...]], 0), image, NT)
    g = gram[...]
    left = jnp.concatenate([g[:cols, :cols], g[cols:, :cols], g[cols:, cols:]], 0)
    split(odd, jnp.concatenate([left, cross], 1), mine, theirs)


def half_of(cols):
    return jax.ShapeDtypeStruct((3 * cols // 2, 2 * cols), jnp.float32)


def first_images(nb, table, odd, tiles, own, twin, other, x, p, gram):
    (count, size, depth), cols = tiles.shape, x.shape[0]
    vmem = pl.BlockSpec(memory_space=pltpu.VMEM)
    smem = pl.BlockSpec(memory_space=pltpu.SMEM)
    return pl.pallas_call(
        first_kernel,
        out_shape=(
            jax.ShapeDtypeStruct(x.shape, jnp.float32),
            jax.ShapeDtypeStruct(x.shape, jnp.float32),
            half_of(cols),
            half_of(cols),
        ),
        in_specs=[smem, smem] + [vmem] * 8,
        out_specs=(vmem,) * 4,
        scratch_shapes=[
            *slab_scratch(count, 2 * cols, size, depth, PER),
            pltpu.VMEM((2 * cols, x.shape[1]), jnp.float32),
        ],
        compiler_params=pltpu.CompilerParams(vmem_limit_bytes=20 * MIB),
        cost_estimate=pl.CostEstimate(flops=10000000000, bytes_accessed=4000000, transcendentals=0),
    )(nb, table, odd, pltpu.with_memory_space_constraint(tiles, pltpu.VMEM), own, twin, other, x, p, gram)


def middle_kernel(sent, x, x_image, p, p_image, packed, zeros):
    zeros[...] = jnp.zeros_like(zeros)
    packed[...] = dot16(jnp.concatenate([x[...], x_image[...], p[...]], 0), p_image[...], NT)


def middle_products(sent, x, x_image, p, p_image):
    vmem = pl.BlockSpec(memory_space=pltpu.VMEM)
    return pl.pallas_call(
        middle_kernel,
        out_shape=(jax.ShapeDtypeStruct((3 * x.shape[0], x.shape[0]), jnp.float32), ZEROS),
        in_specs=[pl.BlockSpec(memory_space=pl.ANY)] + [vmem] * 4,
        out_specs=(vmem, vmem),
        compiler_params=pltpu.CompilerParams(vmem_limit_bytes=4 * MIB),
        cost_estimate=pl.CostEstimate(flops=1500000000, bytes_accessed=3000000, transcendentals=0),
    )(sent, x, x_image, p, p_image)


def second_kernel(
    nb, table, odd, tiles, own, twin, other, x, r, p, middle, quotient, parts, r_image, mine, theirs, low, high, ends
):
    count, size = tiles.shape[0], tiles.shape[1]
    fill_slabs(low, high, (own, twin, other), count, size)
    multiply_tiles(nb, table, tiles, low, high, ends, r_image)
    cross = dot16(jnp.concatenate([x[...], r[...], p[...]], 0), r_image[...], NT)
    c = x.shape[0]
    xp, ip, pp = middle[:c], middle[c : 2 * c], middle[2 * c :]
    rp = ip - dot32(quotient[...], xp, TN)
    split(odd, jnp.concatenate([cross, jnp.concatenate([xp, rp, pp], 0)], 1), mine, theirs)


def second_images(nb, table, odd, tiles, own, twin, other, x, r, p, middle, quotient, parts):
    (count, size, depth), cols = tiles.shape, x.shape[0]
    vmem = pl.BlockSpec(memory_space=pltpu.VMEM)
    smem = pl.BlockSpec(memory_space=pltpu.SMEM)
    return pl.pallas_call(
        second_kernel,
        out_shape=(
            jax.ShapeDtypeStruct(x.shape, jnp.float32),
            half_of(cols),
            half_of(cols),
        ),
        in_specs=[smem, smem] + [vmem] * 10 + [pl.BlockSpec(memory_space=pl.ANY)],
        out_specs=(vmem,) * 3,
        scratch_shapes=slab_scratch(count, cols, size, depth, PER),
        compiler_params=pltpu.CompilerParams(vmem_limit_bytes=20 * MIB),
        cost_estimate=pl.CostEstimate(flops=10000000000, bytes_accessed=4000000, transcendentals=0),
    )(nb, table, odd, pltpu.with_memory_space_constraint(tiles, pltpu.VMEM), own, twin, other, x, r, p, middle, quotient, parts)


def cholesky_inverse(a):
    n, step = a.shape[0], 8
    rows = lax.broadcasted_iota(jnp.int32, (step, 2 * n), 0)
    lanes = lax.broadcasted_iota(jnp.int32, (n, n), 1)
    unit = (lanes == lax.broadcasted_iota(jnp.int32, (n, n), 0)).astype(jnp.float32)
    m = jnp.concatenate([a, unit], 1)
    bands = [m[i : i + step] for i in range(0, n, step)]
    pivots = []
    for at in range(n // step):
        live = range(at, n // step)
        columns = [
            {t: jnp.broadcast_to(bands[t][:, at * step + i : at * step + i + 1], (step, 2 * n)) for t in live}
            for i in range(step)
        ]
        for i in range(step):
            pivot = columns[i][at][i : i + 1]
            pivots.append(pivot)
            over = 1.0 / pivot
            row = bands[at][i : i + 1]
            factor = {t: columns[i][t] * over for t in live}
            factor[at] = jnp.where(rows > i, factor[at], 0.0)
            for later in range(i + 1, step):
                entry = columns[later][at][i : i + 1]
                for t in live:
                    columns[later][t] = columns[later][t] - factor[t] * entry
            for t in live:
                bands[t] = bands[t] - factor[t] * row
    scale = jnp.concatenate(pivots, 0)
    return (jnp.concatenate(bands, 0) * (1.0 / jnp.sqrt(scale)))[:, n:]


def residual_kernel(odd, mine, theirs, x, x_image, packed, quotient, inverse, residual, rounded):
    cols = x.shape[0]
    packed[...] = join(odd, mine[...], theirs[...])
    gram, cross = packed[:cols, :cols], packed[:cols, cols:]
    w = cholesky_inverse(gram)
    inverse[...] = w
    q = dot32(w, dot32(w, cross, NN), TN)
    quotient[...] = q
    r = x_image[...] - dot32(q, x[...], TN)
    residual[...] = r
    rounded[...] = r.astype(jnp.bfloat16)


def residual_of(odd, mine, theirs, x, x_image):
    cols = x.shape[0]
    vmem = pl.BlockSpec(memory_space=pltpu.VMEM)
    square = jax.ShapeDtypeStruct((cols, cols), jnp.float32)
    return pl.pallas_call(
        residual_kernel,
        out_shape=(
            jax.ShapeDtypeStruct((3 * cols, 2 * cols), jnp.float32),
            square,
            square,
            jax.ShapeDtypeStruct(x.shape, jnp.float32),
            jax.ShapeDtypeStruct(x.shape, jnp.bfloat16),
        ),
        in_specs=[vmem] * 5,
        out_specs=(vmem,) * 5,
        compiler_params=pltpu.CompilerParams(vmem_limit_bytes=4 * MIB),
        cost_estimate=pl.CostEstimate(flops=3000000000, bytes_accessed=3000000, transcendentals=0),
    )(odd, mine, theirs, x, x_image)


def factor_kernel(total, packed, quotient, x_inverse, parts):
    c = quotient.shape[0]
    q = quotient[...]
    xx, px, pp = packed[:c, :c], packed[c : 2 * c, :c], packed[2 * c :, :c]
    xi, ii, pi = packed[:c, c:], packed[c : 2 * c, c:], packed[2 * c :, c:]
    rx = xi.T - dot32(q, xx, TN)
    ri = ii - dot32(q, xi, TN)
    rr = ri - dot32(rx, q, NN)
    pr = pi - dot32(px, q, NN)
    scale = 1.0 / total
    w1 = x_inverse[...] * (total**0.5)
    l21, l31 = dot32(rx * scale, w1, NT), dot32(px * scale, w1, NT)
    w2 = cholesky_inverse(rr * scale - dot32(l21, l21, NT))
    l32 = dot32(pr * scale - dot32(l31, l21, NT), w2, NT)
    last = pp * scale - dot32(l31, l31, NT) - dot32(l32, l32, NT)
    for at, part in enumerate((w1, w2, l21, l31, l32, last, ri)):
        parts[at] = part


def factor(total, packed, quotient, x_inverse):
    c = quotient.shape[0]
    vmem = pl.BlockSpec(memory_space=pltpu.VMEM)
    return pl.pallas_call(
        functools.partial(factor_kernel, total),
        out_shape=jax.ShapeDtypeStruct((7, c, c), jnp.float32),
        in_specs=[vmem] * 3,
        out_specs=vmem,
        compiler_params=pltpu.CompilerParams(vmem_limit_bytes=4 * MIB),
        cost_estimate=pl.CostEstimate(flops=2000000000, bytes_accessed=3000000, transcendentals=0),
    )(packed, quotient, x_inverse)


def inverse_kernel(sent, parts, inverse, zeros):
    zeros[...] = jnp.zeros_like(zeros)
    w1, w2, l21, l31, l32 = parts[0], parts[1], parts[2], parts[3], parts[4]
    w21 = -dot32(w2, dot32(l21, w1, NN), NN)
    below = dot32(l31, w1, NN) + dot32(l32, w21, NN)
    beside = dot32(l32, w2, NN)
    w3 = cholesky_inverse(parts[5])
    w3_below = -dot32(w3, jnp.concatenate([below, beside], 1), NN)
    zero = jnp.zeros_like(w1)
    inverse[...] = jnp.concatenate(
        [
            jnp.concatenate([w1, zero, zero], 1),
            jnp.concatenate([w21, w2, zero], 1),
            jnp.concatenate([w3_below, w3], 1),
        ],
        0,
    )


def inverse_of(sent, parts):
    width = 3 * parts.shape[1]
    vmem = pl.BlockSpec(memory_space=pltpu.VMEM)
    return pl.pallas_call(
        inverse_kernel,
        out_shape=(jax.ShapeDtypeStruct((width, width), jnp.float32), ZEROS),
        in_specs=[pl.BlockSpec(memory_space=pl.ANY), vmem],
        out_specs=(vmem, vmem),
        compiler_params=pltpu.CompilerParams(vmem_limit_bytes=4 * MIB),
        cost_estimate=pl.CostEstimate(flops=2000000000, bytes_accessed=3000000, transcendentals=0),
    )(sent, parts)


def basis_kernel(extra, sent, inverse, x, r, p, x_image, r_image, p_image, *rest):
    basis, basis_image, zeros = rest[extra:]
    zeros[...] = jnp.zeros_like(zeros)
    w = inverse[...]
    basis[...] = dot16(w, jnp.concatenate([x[...], r[...], p[...]], 0), NN)
    basis_image[...] = dot16(w, jnp.concatenate([x_image[...], r_image[...], p_image[...]], 0), NN)


def bases(part, parts, sent, inverse, blocks, done):
    width, rows = inverse.shape[0], blocks[0].shape[1]
    cols = blocks[0].shape[0]
    tile = 768
    steps = rows // tile // parts
    first = part * steps
    whole = pl.BlockSpec(memory_space=pl.ANY)
    block = pl.BlockSpec((cols, tile), lambda i: (0, first + i))
    out = pl.BlockSpec((width, tile), lambda i: (0, first + i))
    return pl.pallas_call(
        functools.partial(basis_kernel, len(done)),
        grid=(steps,),
        out_shape=(jax.ShapeDtypeStruct((width, rows), jnp.float32),) * 2 + (ZEROS,),
        in_specs=[whole, pl.BlockSpec((width, width), lambda i: (0, 0))] + [block] * 6 + [whole] * len(done),
        out_specs=(out, out, pl.BlockSpec((8, 128), lambda i: (0, 0))),
        input_output_aliases={8 + i: i for i in range(len(done))},
        compiler_params=pltpu.CompilerParams(vmem_limit_bytes=12 * MIB),
        cost_estimate=pl.CostEstimate(flops=2000000000, bytes_accessed=3000000, transcendentals=0),
    )(sent, inverse, *blocks, *done)


def project_kernel(total, odd, inverse, packed, parts, mine, theirs, projected):
    c = parts.shape[1]
    left = jnp.concatenate([packed[:c, c:], parts[6], packed[2 * c :, c:]], 0)
    w = inverse[...]
    cross = jnp.concatenate([left, join(odd, mine[...], theirs[...])], 1)
    projected[...] = dot16(dot16(w, cross, NN), w, NT) * (1.0 / total)


def project(total, odd, inverse, packed, parts, mine, theirs):
    vmem = pl.BlockSpec(memory_space=pltpu.VMEM)
    return pl.pallas_call(
        functools.partial(project_kernel, total),
        out_shape=jax.ShapeDtypeStruct(inverse.shape, jnp.float32),
        in_specs=[vmem] * 6,
        out_specs=vmem,
        compiler_params=pltpu.CompilerParams(vmem_limit_bytes=20 * MIB),
    )(odd, inverse, packed, parts, mine, theirs)


def shards(sub, dom, tile_blocks, neighbours, send_groups, block_x, block_p):
    devices = sub * dom
    count, rows, cols = tile_blocks.shape[0], block_x.shape[0], block_x.shape[1]
    total = float(rows * devices)
    x, p = block_x.T, block_p.T
    lists = jnp.pad(send_groups.astype(jnp.bfloat16)[None], ((0, 2 * cols - 1), (0, 128 - 2 * count)))
    both = jnp.concatenate([jnp.concatenate([x, p], 0).astype(jnp.bfloat16), lists], 1)
    odd = jnp.broadcast_to(lax.axis_index("sub") % 2, (8, 2 * cols)).astype(jnp.float32)
    twin, other = neighbour_blocks(both, sub, devices)
    twin_list = twin[0, rows : rows + 2 * count].astype(jnp.int32) + count
    other_list = other[0, rows : rows + 2 * count].astype(jnp.int32) + 2 * count
    first_half = odd[0, :count] > 0
    table = jnp.concatenate(
        [
            jnp.where(first_half, twin_list[count:], other_list[count:]),
            jnp.arange(count, dtype=jnp.int32),
            jnp.where(first_half, other_list[:count], twin_list[:count]),
        ]
    )
    tiles, gram = load(odd, tile_blocks, x, p)
    x_image, p_image, *halves = first_images(neighbours, table, odd, tiles, both, twin, other, x, p, gram)
    made = {}

    def step(name, make):
        def run(sent):
            *values, zeros = make(sent)
            made[name] = values
            return zeros

        return run

    halves = all_sum(
        *halves, sub, dom, [step("middle", lambda sent: middle_products(sent, x, x_image, p, p_image))]
    )
    packed, quotient, x_inverse, residual, r_round = residual_of(odd, *halves, x, x_image)
    r_twin, r_other = neighbour_blocks(r_round, sub, devices)
    parts = factor(total, packed, quotient, x_inverse)
    r_image, *halves = second_images(
        neighbours, table, odd, tiles, r_round, r_twin, r_other, x, residual, p, made["middle"][0], quotient, parts
    )
    blocks = (x, residual, p, x_image, r_image, p_image)
    made["bases"] = []
    pieces = 4
    work = [
        step("inverse", lambda sent: inverse_of(sent, parts)),
    ]
    for piece in range(pieces):
        work.append(
            step(
                "bases",
                lambda sent, piece=piece: bases(piece, pieces, sent, made["inverse"][0], blocks, made["bases"]),
            )
        )
    halves = all_sum(*halves, sub, dom, work)
    basis, basis_image = made["bases"]
    projected = project(total, odd, made["inverse"][0], packed, parts, *halves)
    return basis.T, basis_image.T, projected


def solution(mesh):
    placed = (
        P(AXES, None, None, None),
        P(AXES, None),
        P(AXES),
        P(AXES, None),
        P(AXES, None),
    )
    return jax.shard_map(
        functools.partial(shards, mesh.shape["sub"], mesh.shape["dom"]),
        mesh=mesh,
        in_specs=placed,
        out_specs=(P(AXES, None), P(AXES, None), P()),
        check_vma=False,
    )
```
